32 devices in a mesh: seq: 16 (over z, y, x), tp: 2 (over core).
Axes of the slice: x: 2, y: 2, z: 4, core: 2. Of those that a mesh axis runs over, the one named last changes fastest.
Arguments:
- tokens: bfloat16 [96, 2048], P('seq', 'tp'), may hold values from -6 to 6
- norm_gain: float32 [2048], replicated, may hold values from 0.25 to 4
- w_query: bfloat16 [2048, 2048], P(None, 'tp'), may hold values from -0.125 to 0.125
- w_key_value: bfloat16 [2, 2048, 1024], P(None, None, 'tp'), may hold values from -0.125 to 0.125
- w_out: bfloat16 [2048, 2048], P('tp'), may hold values from -0.125 to 0.125
- kv_pool: bfloat16 [2, 1792, 16, 1024], P(None, 'seq', None, 'tp'), may hold values from -256 to 256
- slot_owner: int32 [1792, 2], P('seq'), may hold values from -1 to 447, as said below
- slot_dest: int32 [1792], P('seq'), may hold values from -1 to 1791, as said below
- lengths: int32 [24], replicated, may hold values from 1 to 7164, as said below
Outputs:
- attn_out: bfloat16 [96, 2048], P('seq', 'tp')
- kv_moved: bfloat16 [2, 1792, 16, 1024], P(None, 'seq', None, 'tp')
The draws below stay inside these ranges and needn't reach their ends.
Inputs may be any that keep to these rules, and one draw needn't show every extreme that they name: `lengths`: two requests are long, at least 5731 and one of them exactly 7164; the others hold at most 444. `slot_owner`: pages 0 to (lengths[r] + 3) // 16 of every request r are held by exactly one slot each, no other pages by any; a free slot holds (-1, -1). `slot_dest`: -1 where the page stays. Destinations are distinct, each a free slot or a slot whose own page moves. At most 7 slots of one index of seq move to slots of one index of seq, and exactly 7 do for some pair in every draw.
All inputs are finite; a program needn't handle non-finite values.
Results may differ from the reference program's by a relative error of at most 0.024.
The reference program's roundings to bfloat16 on the way (of `normed`, `queries`, `written` and `attended`) count: a program that leaves them out, or rounds other values in their place, can miss the bound.
Values may be sent and summed in bfloat16 or wider, within the bound.
No kernel may reach another device: no remote copies, remote signals or barrier semaphores. Data moves between devices by JAX's collectives and lax.ppermute only.
A program may use at most 128 MiB of HBM per device.

```python
import math
import jax
import jax.numpy as jnp
from jax import lax

D = 2048
HEADS = 16
KV_HEADS = 8
HD = 128
STEPS = 4
PAGE = 16
SLOTS = 112
ROWS = 96
REQS = 24
LONG_MAX = 7164
LONG_MIN = 5731
SHORT_MAX = 444
N_SEQ = 16


def layout(key):
    base_key = jax.random.fold_in(key, 4242)
    pick_key, short_key, long_key, device_key = jax.random.split(base_key, 4)
    slot_total = N_SEQ * SLOTS
    chosen = jax.random.permutation(pick_key, REQS)
    first_long = jnp.minimum(chosen[0], chosen[1])
    second_long = jnp.maximum(chosen[0], chosen[1])
    lengths = jax.random.randint(short_key, (REQS,), 1, SHORT_MAX + 1)
    other_len = jax.random.randint(long_key, (), LONG_MIN, LONG_MAX + 1)
    flip_bit = jax.random.randint(jax.random.fold_in(long_key, 1), (), 0, 2)
    len_first = jnp.where(flip_bit == 0, LONG_MAX, other_len)
    len_second = jnp.where(flip_bit == 0, other_len, LONG_MAX)
    lengths = lengths.at[first_long].set(len_first).at[second_long].set(len_second)
    page_need = (lengths + STEPS - 1) // PAGE + 1
    request_ids = jnp.arange(REQS, dtype=jnp.int32)
    is_long = (request_ids == first_long) | (request_ids == second_long)
    pages_first = page_need[first_long]
    long_total = pages_first + page_need[second_long]
    devices = jax.random.permutation(device_key, N_SEQ)
    slot_major = jnp.arange(slot_total, dtype=jnp.int32)
    logical_dev = slot_major % N_SEQ
    logical_slot = slot_major // N_SEQ
    logical_index = logical_dev * SLOTS + logical_slot
    takes_long = logical_index < long_total
    short_rank = jnp.cumsum(jnp.where(takes_long, 0, 1)) - 1
    short_pages = jnp.where(is_long, 0, page_need)
    page_ends = jnp.cumsum(short_pages)
    short_req = jnp.minimum(jnp.searchsorted(page_ends, short_rank, side='right'), REQS - 1).astype(jnp.int32)
    short_page = short_rank - (page_ends[short_req] - short_pages[short_req])
    has_short = ~takes_long & (short_rank < page_ends[-1])
    long_req = jnp.where(logical_index < pages_first, first_long, second_long)
    long_page = jnp.where(logical_index < pages_first, logical_index, logical_index - pages_first)
    owner_req = jnp.where(takes_long, long_req, jnp.where(has_short, short_req, -1))
    owner_page = jnp.where(takes_long, long_page, jnp.where(has_short, short_page, -1))
    physical = devices[logical_dev] * SLOTS + logical_slot
    owner_table = jnp.full((slot_total, 2), -1, jnp.int32)
    owner_table = owner_table.at[physical].set(jnp.stack([owner_req, owner_page], axis=1).astype(jnp.int32))
    open_grid = (~has_short).reshape(SLOTS, N_SEQ).T
    open_rank = jnp.cumsum(open_grid.astype(jnp.int32), axis=1) - 1
    long_index = jnp.arange(slot_total, dtype=jnp.int32)
    target_dev = long_index % N_SEQ
    target_rank = long_index // N_SEQ
    matches = open_grid[target_dev] & (open_rank[target_dev] == target_rank[:, None])
    target_slot = jnp.argmax(matches.astype(jnp.int32), axis=1).astype(jnp.int32)
    dest_phys = devices[target_dev] * SLOTS + target_slot
    source_phys = devices[long_index // SLOTS] * SLOTS + long_index % SLOTS
    moved = long_index < long_total
    dest_table = jnp.full((slot_total,), -1, jnp.int32).at[source_phys].set(jnp.where(moved, dest_phys, -1).astype(jnp.int32))
    return (lengths.astype(jnp.int32), owner_table, dest_table)


def draw_lengths(key, part):
    return layout(key)[0]


def draw_slot_owner(key, part):
    return layout(key)[1]


def draw_slot_dest(key, part):
    return layout(key)[2]


def draw_kv_pool(key, part):
    pool_shape = (N_SEQ * SLOTS, PAGE, KV_HEADS * HD)
    key_part, value_part = jax.random.split(jax.random.fold_in(key, 515), 2)
    page_keys = 2.0 * jnp.clip(jax.random.normal(key_part, pool_shape), -4.0, 4.0)
    page_values = jnp.clip(jax.random.normal(value_part, pool_shape), -5.0, 5.0)
    return jnp.stack([page_keys, page_values]).astype(jnp.bfloat16)


def steps_of(own_key, extent, cuts, low, high):
    gain = 1.0
    for dim, blocks in cuts:
        heights = jax.random.uniform(jax.random.fold_in(jax.random.fold_in(own_key, 6), dim), (blocks,), jnp.float32, low / len(cuts), high / len(cuts))
        gain = gain * jnp.repeat(jnp.exp(heights), extent[dim] // blocks).reshape((-1,) + (1,) * (len(extent) - 1 - dim))
    return gain


def scatter_about(key, dims, deviation, reach, pieces=(), kind=jnp.bfloat16):
    drawn = deviation * jax.random.normal(key, dims, jnp.float32)
    if pieces:
        drawn = drawn * steps_of(key, dims, pieces, -0.22, 0.18)
    return jnp.clip(drawn, -reach, reach).astype(kind)


def setup_inputs(seed: int = 0) -> dict:
    keys = jax.random.split(jax.random.key(seed), 10)
    return {
        "tokens": scatter_about(keys[0], (ROWS, D), 1.0, 6.0, ((0, 16), (1, 2))),
        "norm_gain": jnp.clip(jnp.exp(jax.random.uniform(keys[1], (D,), jnp.float32, math.log(0.25), math.log(4.0))), 0.25, 4.0),
        "w_query": scatter_about(keys[2], (D, HEADS * HD), D ** -0.5, 0.125, ((1, 2),)),
        "w_key_value": scatter_about(keys[3], (2, D, KV_HEADS * HD), D ** -0.5, 0.125, ((2, 2),)),
        "w_out": scatter_about(keys[4], (HEADS * HD, D), (HEADS * HD) ** -0.5, 0.125, ((0, 2),)),
        "kv_pool": draw_kv_pool(jax.random.fold_in(keys[9], 71), 0),
        "slot_owner": draw_slot_owner(jax.random.fold_in(keys[9], 71), 0),
        "slot_dest": draw_slot_dest(jax.random.fold_in(keys[9], 71), 0),
        "lengths": draw_lengths(jax.random.fold_in(keys[9], 71), 0),
    }


ROPE_BASE = 1000000.0
NEG_FILL = -1e+30
NORM_EPS = 1e-06

def rotate(projected, positions, head_count):
    row_count = projected.shape[0]
    width = projected.shape[1] // head_count
    half_width = width // 2
    heads_view = projected.reshape(row_count, head_count, width)
    frequency = ROPE_BASE ** (-jnp.arange(half_width, dtype=jnp.float32) * 2.0 / width)
    angles = positions.astype(jnp.float32)[:, None] * frequency[None, :]
    cosine = jnp.cos(angles)[:, None, :]
    sine_part = jnp.sin(angles)[:, None, :]
    lower_half = heads_view[:, :, :half_width]
    upper_half = heads_view[:, :, half_width:]
    turned = jnp.concatenate([lower_half * cosine - upper_half * sine_part, upper_half * cosine + lower_half * sine_part], axis=2)
    return turned.reshape(row_count, head_count * width)

def reference(tokens, norm_gain, w_query, w_key_value, w_out, kv_pool, slot_owner, slot_dest, lengths):
    row_total = tokens.shape[0]
    row_index = jnp.arange(row_total, dtype=jnp.int32)
    positions = lengths[row_index // STEPS] + row_index % STEPS
    widened = tokens.astype(jnp.float32)
    mean_square = lax.optimization_barrier(jnp.mean(widened * widened, axis=1, keepdims=True))
    normed = (widened * lax.rsqrt(mean_square + NORM_EPS) * norm_gain.astype(jnp.float32)[None, :]).astype(jnp.bfloat16)
    queries = jnp.dot(normed, w_query, preferred_element_type=jnp.float32)
    key_proj = jnp.dot(normed, w_key_value[0], preferred_element_type=jnp.float32)
    value_proj = jnp.dot(normed, w_key_value[1], preferred_element_type=jnp.float32)
    queries = rotate(queries, positions, HEADS).astype(jnp.bfloat16)
    new_keys = rotate(key_proj, positions, KV_HEADS).astype(jnp.bfloat16)
    new_values = value_proj.astype(jnp.bfloat16)
    slot_total = kv_pool.shape[1]
    page_size = kv_pool.shape[2]
    owner_req = slot_owner[:, 0]
    owner_page = slot_owner[:, 1]
    occupied = owner_req >= 0
    safe_req = jnp.where(occupied, owner_req, 0)
    base_len = lengths[safe_req]
    offset = jnp.arange(page_size, dtype=jnp.int32)
    position = owner_page[:, None] * page_size + offset[None, :]
    step_of = position - base_len[:, None]
    is_new = occupied[:, None] & (step_of >= 0) & (step_of < STEPS)
    source_row = jnp.where(is_new, safe_req[:, None] * STEPS + step_of, 0).astype(jnp.int32)
    fresh_rows = jnp.stack([new_keys[source_row], new_values[source_row]])
    written = jnp.where(is_new[None, :, :, None], fresh_rows, kv_pool)
    group_size = HEADS // KV_HEADS
    step_ids = jnp.arange(STEPS, dtype=jnp.int32)
    visible = occupied[:, None, None] & (position[:, None, :] <= base_len[:, None, None] + step_ids[None, :, None])
    visible = visible[:, :, None, :]
    member = owner_req[None, :] == jnp.arange(REQS, dtype=jnp.int32)[:, None]
    segment = jnp.where(occupied, owner_req, REQS).astype(jnp.int32)
    slot_queries = queries.reshape(REQS, STEPS, KV_HEADS, group_size, HD)[safe_req]
    slot_queries = jnp.transpose(slot_queries, (2, 0, 1, 3, 4))
    page_keys = jnp.transpose(written[0].reshape(slot_total, page_size, KV_HEADS, HD), (2, 0, 1, 3))
    page_values = jnp.transpose(written[1].reshape(slot_total, page_size, KV_HEADS, HD), (2, 0, 1, 3))

    def one_head(head_parts):
        head_queries, head_keys, head_values = head_parts
        scores = jnp.einsum('stgd,spd->stgp', head_queries.astype(jnp.float32), head_keys.astype(jnp.float32)) * HD ** (-0.5)
        scores = jnp.where(visible, scores, NEG_FILL)
        slot_top = lax.optimization_barrier(jnp.max(scores, axis=3)).reshape(slot_total, -1)
        req_top = lax.optimization_barrier(jnp.max(jnp.where(member[:, :, None], slot_top[None, :, :], NEG_FILL), axis=1))
        slot_ref = req_top[safe_req].reshape(slot_total, STEPS, group_size, 1)
        weights = jnp.where(visible, jnp.exp(scores - slot_ref), 0.0)
        totals = jax.ops.segment_sum(lax.optimization_barrier(jnp.sum(weights, axis=3)), segment, num_segments=REQS + 1)[:REQS]
        rounded = lax.optimization_barrier(weights.astype(jnp.bfloat16)).astype(jnp.float32)
        products = jnp.einsum('stgp,spd->stgd', rounded, head_values.astype(jnp.float32))
        sums = jax.ops.segment_sum(products, segment, num_segments=REQS + 1)[:REQS]
        return sums / totals[..., None]
    per_head = lax.map(one_head, (slot_queries, page_keys, page_values))
    attended = jnp.transpose(per_head, (1, 2, 0, 3, 4)).reshape(row_total, HEADS * HD).astype(jnp.bfloat16)
    attn_out = jnp.dot(attended, w_out, preferred_element_type=jnp.float32).astype(jnp.bfloat16)
    moving = slot_dest >= 0
    slot_ids = jnp.arange(slot_total, dtype=jnp.int32)
    source_for = jnp.full((slot_total,), -1, jnp.int32).at[jnp.where(moving, slot_dest, slot_total)].set(slot_ids, mode='drop')
    landed = source_for >= 0
    incoming = written[:, jnp.where(landed, source_for, 0)]
    kv_moved = jnp.where(landed[None, :, None, None], incoming, jnp.where(moving[None, :, None, None], jnp.zeros_like(written), written))
    return (attn_out, kv_moved)
```

```python
import functools

import jax
import jax.numpy as jnp
from jax import lax
from jax.experimental import pallas as pl
from jax.experimental.pallas import tpu as pltpu
from jax.sharding import PartitionSpec as P

HD = 128
STEPS = 4
STAT_PARTS = 3

ROPE_BASE = 1000000.0
NEG_FILL = -1e30
NORM_EPS = 1e-06


def rotate(projected, positions, head_count):
    row_count = projected.shape[0]
    width = projected.shape[1] // head_count
    half_width = width // 2
    heads_view = projected.reshape(row_count, head_count, width)
    frequency = ROPE_BASE ** (-jnp.arange(half_width, dtype=jnp.float32) * 2.0 / width)
    angles = positions.astype(jnp.float32)[:, None] * frequency[None, :]
    cosine = jnp.cos(angles)[:, None, :]
    sine_part = jnp.sin(angles)[:, None, :]
    lower_half = heads_view[:, :, :half_width]
    upper_half = heads_view[:, :, half_width:]
    turned = jnp.concatenate(
        [
            lower_half * cosine - upper_half * sine_part,
            upper_half * cosine + lower_half * sine_part,
        ],
        axis=2,
    )
    return turned.reshape(row_count, head_count * width)


def project_rows(token_block, norm_gain, w_query, w_key_value, lengths):
    row_count = token_block.shape[0]
    row_index = jnp.arange(row_count, dtype=jnp.int32)
    positions = lengths[row_index // STEPS] + row_index % STEPS
    widened = token_block.astype(jnp.float32)
    mean_square = jnp.mean(widened * widened, axis=1, keepdims=True)
    normed = (widened * lax.rsqrt(mean_square + NORM_EPS) * norm_gain[None, :]).astype(jnp.bfloat16)
    queries = jnp.dot(normed, w_query, preferred_element_type=jnp.float32)
    keyval = jnp.einsum("rd,cde->cre", normed, w_key_value, preferred_element_type=jnp.float32)
    queries = rotate(queries, positions, w_query.shape[1] // HD).astype(jnp.bfloat16)
    fresh_key = rotate(keyval[0], positions, w_key_value.shape[2] // HD).astype(jnp.bfloat16)
    fresh_value = keyval[1].astype(jnp.bfloat16)
    return queries, fresh_key, fresh_value


def pack_body(slot_count, seq_count, capacity, dest_ref, owner_ref, pool_ref, out_ref, meta_ref, count_ref, sem):
    def clear(i, carry):
        meta_ref[0, i] = -1
        meta_ref[1, i] = -1
        meta_ref[2, i] = 0
        return carry

    lax.fori_loop(0, seq_count * capacity, clear, 0)

    def reset(i, carry):
        count_ref[i] = 0
        return carry

    lax.fori_loop(0, seq_count, reset, 0)

    def send(slot, total):
        dest = dest_ref[slot]
        moving = dest >= 0

        @pl.when(moving)
        def _():
            target = dest // slot_count
            rank = count_ref[target]
            count_ref[target] = rank + 1
            place = target * capacity + rank
            meta_ref[0, place] = dest - target * slot_count
            meta_ref[1, place] = owner_ref[slot * 2]
            meta_ref[2, place] = owner_ref[slot * 2 + 1]
            pltpu.make_async_copy(pool_ref.at[:, slot], out_ref.at[place], sem).start()

        return total + moving.astype(jnp.int32)

    total = lax.fori_loop(0, slot_count, send, 0)

    def finish(i, carry):
        pltpu.make_async_copy(pool_ref.at[:, 0], out_ref.at[0], sem).wait()
        return carry

    lax.fori_loop(0, total, finish, 0)


def pack_pages(kv_pool, slot_dest, slot_owner, seq_count):
    slot_count, page_size, width = kv_pool.shape[1:]
    capacity = -(-slot_count // seq_count)
    places = seq_count * capacity
    return pl.pallas_call(
        functools.partial(pack_body, slot_count, seq_count, capacity),
        out_shape=(
            jax.ShapeDtypeStruct((places, 2, page_size, width), kv_pool.dtype),
            jax.ShapeDtypeStruct((3, places), jnp.int32),
        ),
        in_specs=[
            pl.BlockSpec(memory_space=pltpu.SMEM),
            pl.BlockSpec(memory_space=pltpu.SMEM),
            pl.BlockSpec(memory_space=pl.ANY),
        ],
        out_specs=(
            pl.BlockSpec(memory_space=pl.ANY),
            pl.BlockSpec(memory_space=pltpu.SMEM),
        ),
        scratch_shapes=[pltpu.SMEM((seq_count,), jnp.int32), pltpu.SemaphoreType.DMA],
        name="pack_pages",
    )(slot_dest, slot_owner.reshape(-1), kv_pool)


def place_body(
    slot_count, places, page_size,
    dest_ref, owner_ref, meta_ref, length_ref, pool_ref, arrived_ref, key_ref, value_ref,
    out_ref, landed_ref, patch_ref, zero_ref, sem,
):
    zero_ref[...] = jnp.zeros_like(zero_ref)

    def reset(i, carry):
        landed_ref[i] = 0
        return carry

    lax.fori_loop(0, slot_count, reset, 0)

    def note_patch(count, slot, req, page):
        first = length_ref[jnp.maximum(req, 0)] - page * page_size
        hit = (req >= 0) & (first > -STEPS) & (first < page_size)

        @pl.when(hit)
        def _():
            patch_ref[0, count] = slot
            patch_ref[1, count] = req
            patch_ref[2, count] = first

        return count + hit.astype(jnp.int32)

    def land(place, count):
        slot = meta_ref[0, place]

        @pl.when(slot >= 0)
        def _():
            landed_ref[slot] = 1
            pltpu.make_async_copy(arrived_ref.at[place], out_ref.at[:, slot], sem).start()

        return note_patch(count, slot, jnp.where(slot >= 0, meta_ref[1, place], -1), meta_ref[2, place])

    count = lax.fori_loop(0, places, land, 0)

    def keep(slot, count):
        vacant = landed_ref[slot] == 0
        stays = (dest_ref[slot] < 0) & vacant

        @pl.when(stays)
        def _():
            pltpu.make_async_copy(pool_ref.at[:, slot], out_ref.at[:, slot], sem).start()

        @pl.when((dest_ref[slot] >= 0) & vacant)
        def _():
            pltpu.make_async_copy(zero_ref, out_ref.at[:, slot], sem).start()

        return note_patch(
            count, slot, jnp.where(stays, owner_ref[slot * 2], -1), owner_ref[slot * 2 + 1]
        )

    count = lax.fori_loop(0, slot_count, keep, count)
    pltpu.make_async_copy(pool_ref, out_ref, sem).wait()
    entry = lax.broadcasted_iota(jnp.int32, (page_size, out_ref.shape[3]), 0)

    def patch(i, carry):
        slot = patch_ref[0, i]
        req = patch_ref[1, i]
        first = patch_ref[2, i]
        for which, fresh_ref in ((0, key_ref), (1, value_ref)):
            page = out_ref[which, slot].astype(jnp.float32)
            for step in range(STEPS):
                fresh = fresh_ref[pl.ds(req * STEPS + step, 1), :]
                page = jnp.where(entry == first + step, fresh, page)
            out_ref[which, slot] = page.astype(out_ref.dtype)
        return carry

    lax.fori_loop(0, count, patch, 0)


def place_pages(kv_pool, arrived, meta, slot_dest, slot_owner, lengths, key_new, value_new):
    slot_count, page_size, width = kv_pool.shape[1:]
    places = arrived.shape[0]
    smem = pl.BlockSpec(memory_space=pltpu.SMEM)
    hbm = pl.BlockSpec(memory_space=pl.ANY)
    vmem = pl.BlockSpec(memory_space=pltpu.VMEM)
    return pl.pallas_call(
        functools.partial(place_body, slot_count, places, page_size),
        out_shape=jax.ShapeDtypeStruct(kv_pool.shape, kv_pool.dtype),
        in_specs=[smem, smem, smem, smem, hbm, hbm, vmem, vmem],
        out_specs=vmem,
        scratch_shapes=[
            pltpu.SMEM((slot_count,), jnp.int32),
            pltpu.SMEM((3, slot_count), jnp.int32),
            pltpu.VMEM((2, page_size, width), kv_pool.dtype),
            pltpu.SemaphoreType.DMA,
        ],
        compiler_params=pltpu.CompilerParams(vmem_limit_bytes=32 * 2**20),
        name="place_pages",
    )(
        slot_dest, slot_owner.reshape(-1), meta, lengths, kv_pool, arrived,
        key_new.astype(jnp.float32), value_new.astype(jnp.float32),
    )


def split_parts(value):
    parts = []
    for _ in range(STAT_PARTS):
        part = value.astype(jnp.bfloat16).astype(jnp.float32)
        parts.append(part)
        value = value - part
    return parts


def attend_body(
    kv_count, group_size, seq_count,
    index_ref, query_ref, key_new_ref, value_new_ref, key_req_ref, pool_ref, out_ref,
):
    rows = query_ref.shape[0]
    entries = key_req_ref.shape[1]
    q_count = kv_count * group_size
    stack = rows * group_size
    row = lax.broadcasted_iota(jnp.int32, (stack, 1), 0) % rows
    row_req = row // STEPS
    new_row = lax.broadcasted_iota(jnp.int32, (stack, rows), 1)
    mine = (row_req % seq_count) == index_ref[0]
    new_mask = (new_row // STEPS == row_req) & (new_row <= row) & mine
    lane = lax.broadcasted_iota(jnp.int32, (rows, HD), 1)
    stats = jnp.zeros((rows, HD), jnp.float32)
    for head in range(kv_count):
        cols = slice(head * HD, (head + 1) * HD)
        query = jnp.concatenate(
            [
                query_ref[:, (head * group_size + g) * HD : (head * group_size + g + 1) * HD]
                for g in range(group_size)
            ],
            axis=0,
        )
        contract = (((1,), (1,)), ((), ()))
        old = lax.dot_general(
            query, pool_ref[0, :, cols], contract, preferred_element_type=jnp.float32
        ) * HD ** (-0.5)
        fresh = lax.dot_general(
            query, key_new_ref[:, cols], contract, preferred_element_type=jnp.float32
        ) * HD ** (-0.5)
        old_mask = key_req_ref[...] == row_req
        old = jnp.where(old_mask, old, NEG_FILL)
        fresh = jnp.where(new_mask, fresh, NEG_FILL)
        top = jnp.maximum(
            jnp.max(old, axis=1, keepdims=True), jnp.max(fresh, axis=1, keepdims=True)
        )
        old = jnp.where(old_mask, jnp.exp(old - top), 0.0)
        fresh = jnp.where(new_mask, jnp.exp(fresh - top), 0.0)
        total = jnp.sum(old, axis=1, keepdims=True) + jnp.sum(fresh, axis=1, keepdims=True)
        summed = jnp.dot(
            old.astype(jnp.bfloat16), pool_ref[1, :, cols], preferred_element_type=jnp.float32
        ) + jnp.dot(
            fresh.astype(jnp.bfloat16), value_new_ref[:, cols], preferred_element_type=jnp.float32
        )
        summed = summed / jnp.where(total > 0.0, total, 1.0)
        parts = split_parts(top) + split_parts(total)
        for g in range(group_size):
            at = head * group_size + g
            own = slice(g * rows, (g + 1) * rows)
            out_ref[:, at * HD : (at + 1) * HD] = summed[own].astype(out_ref.dtype)
            for k, part in enumerate(parts):
                stats = jnp.where(lane == k * q_count + at, part[own], stats)
    out_ref[:, q_count * HD :] = stats.astype(out_ref.dtype)


def attend(my_index, seq_count, queries, key_new, value_new, key_req, kv_pool):
    slot_count, page_size, width = kv_pool.shape[1:]
    kv_count = width // HD
    rows, q_width = queries.shape
    vmem = pl.BlockSpec(memory_space=pltpu.VMEM)
    return pl.pallas_call(
        functools.partial(attend_body, kv_count, q_width // width, seq_count),
        out_shape=jax.ShapeDtypeStruct((rows, q_width + HD), jnp.bfloat16),
        in_specs=[pl.BlockSpec(memory_space=pltpu.SMEM)] + [vmem] * 5,
        out_specs=vmem,
        compiler_params=pltpu.CompilerParams(vmem_limit_bytes=40 * 2**20),
        name="attend",
    )(
        my_index.reshape(1).astype(jnp.int32), queries, key_new, value_new, key_req,
        kv_pool.reshape(2, slot_count * page_size, width),
    )


def local(tokens, norm_gain, w_query, w_key_value, w_out, kv_pool, slot_owner, slot_dest, lengths):
    seq_count = lax.axis_size("seq")
    my_index = lax.axis_index("seq")
    row_count = tokens.shape[0]
    page_size = kv_pool.shape[2]
    q_width = w_query.shape[1]
    q_count = q_width // HD
    slot_count = kv_pool.shape[1]

    outgoing, meta = pack_pages(kv_pool, slot_dest, slot_owner, seq_count)
    places = outgoing.shape[0]
    own_tokens = lax.all_gather(tokens, "tp", axis=1, tiled=True)
    all_tokens = lax.all_gather(own_tokens, "seq", axis=0, tiled=True)
    arrived = lax.all_to_all(outgoing, "seq", split_axis=0, concat_axis=0, tiled=True)
    arrived_meta = lax.all_to_all(meta, "seq", split_axis=1, concat_axis=1, tiled=True)

    queries, key_new, value_new = project_rows(all_tokens, norm_gain, w_query, w_key_value, lengths)
    owner_req = slot_owner[:, 0]
    base_len = lengths[jnp.maximum(owner_req, 0)]
    position = slot_owner[:, 1][:, None] * page_size + jnp.arange(page_size, dtype=jnp.int32)[None, :]
    key_req = jnp.where(position < base_len[:, None], owner_req[:, None], -1)
    payload = attend(
        my_index, seq_count, queries, key_new, value_new, key_req.reshape(1, -1), kv_pool
    )
    payload = lax.all_to_all(
        payload.reshape(seq_count, row_count, -1), "seq", split_axis=0, concat_axis=0, tiled=True
    ).astype(jnp.float32)
    stats = payload[:, :, q_width : q_width + 2 * STAT_PARTS * q_count]
    stats = stats.reshape(seq_count, row_count, 2, STAT_PARTS, q_count)
    stats = stats[:, :, :, 0] + stats[:, :, :, 1] + stats[:, :, :, 2]
    tops, sums = stats[:, :, 0], stats[:, :, 1]
    share = sums * jnp.exp(tops - jnp.max(tops, axis=0, keepdims=True))
    share = share / jnp.sum(share, axis=0, keepdims=True)
    outs = payload[:, :, :q_width].reshape(seq_count, row_count, q_count, HD)
    attended = jnp.sum(outs * share[..., None], axis=0).reshape(row_count, q_width)
    partial_out = jnp.dot(attended.astype(jnp.bfloat16), w_out, preferred_element_type=jnp.float32)
    attn_out = lax.psum_scatter(
        partial_out.astype(jnp.bfloat16), "tp", scatter_dimension=1, tiled=True
    )
    kv_moved = place_pages(
        kv_pool, arrived, arrived_meta, slot_dest, slot_owner, lengths, key_new, value_new
    )
    return (attn_out, kv_moved)


def solution(mesh):
    in_specs = (
        P("seq", "tp"),
        P(),
        P(None, "tp"),
        P(None, None, "tp"),
        P("tp", None),
        P(None, "seq", None, "tp"),
        P("seq", None),
        P("seq"),
        P(),
    )
    out_specs = (P("seq", "tp"), P(None, "seq", None, "tp"))
    return jax.shard_map(local, mesh=mesh, in_specs=in_specs, out_specs=out_specs, check_vma=False)
```

```python
import functools

import jax
import jax.numpy as jnp
import numpy as np
from jax import lax
from jax.experimental import pallas as pl
from jax.experimental.pallas import tpu as pltpu
from jax.sharding import PartitionSpec as P

HD = 128
STEPS = 4
STAT_PARTS = 3
CHUNK_ROWS = 8
MOST_VMEM = 60 * 2**20
LANES = 128
QUOTIENT_SHIFT = 20

ROPE_BASE = 1000000.0
NEG_FILL = -1e30
NORM_EPS = 1e-06


def rotate(projected, positions, head_count):
    row_count = projected.shape[0]
    width = projected.shape[1] // head_count
    half_width = width // 2
    heads_view = projected.reshape(row_count, head_count, width)
    frequency = ROPE_BASE ** (-jnp.arange(half_width, dtype=jnp.float32) * 2.0 / width)
    angles = positions.astype(jnp.float32)[:, None] * frequency[None, :]
    cosine = jnp.cos(angles)[:, None, :]
    sine_part = jnp.sin(angles)[:, None, :]
    lower_half = heads_view[:, :, :half_width]
    upper_half = heads_view[:, :, half_width:]
    turned = jnp.concatenate(
        [
            lower_half * cosine - upper_half * sine_part,
            upper_half * cosine + lower_half * sine_part,
        ],
        axis=2,
    )
    return turned.reshape(row_count, head_count * width)


def row_ids(row, row_count):
    inner = row % CHUNK_ROWS
    return (row // CHUNK_ROWS) * row_count + inner, inner < row_count


def project_rows(token_block, row_count, norm_gain, w_query, w_key_value, lengths):
    row, held = row_ids(np.arange(token_block.shape[0], dtype=np.int32), row_count)
    row = np.where(held, row, 0)
    positions = length_of(lengths, jnp.asarray(row // STEPS)) + jnp.asarray(row % STEPS)
    widened = token_block.astype(jnp.float32)
    mean_square = jnp.mean(widened * widened, axis=1, keepdims=True)
    normed = (widened * lax.rsqrt(mean_square + NORM_EPS) * norm_gain[None, :]).astype(jnp.bfloat16)
    queries = jnp.dot(normed, w_query, preferred_element_type=jnp.float32)
    keyval = jnp.einsum("rd,cde->cre", normed, w_key_value, preferred_element_type=jnp.float32)
    queries = rotate(queries, positions, w_query.shape[1] // HD).astype(jnp.bfloat16)
    fresh_key = rotate(keyval[0], positions, w_key_value.shape[2] // HD).astype(jnp.bfloat16)
    fresh_value = keyval[1].astype(jnp.bfloat16)
    return queries, fresh_key, fresh_value


def note_body(row_count, stride, token_ref, dest_ref, owner_ref, out_ref, page_ref):
    width = token_ref.shape[1]
    slot_count = dest_ref.shape[1]
    page_ref[...] = jnp.zeros_like(page_ref)
    page_ref[:row_count, :] = token_ref[...].astype(jnp.float32)
    per_row = width // stride
    values = (dest_ref[...], owner_ref[0:1, :], owner_ref[1:2, :])
    for k, value in enumerate(values):
        for part, digit in enumerate(((value + 1) >> 7, (value + 1) & 127)):
            field = 2 * k + part
            row = row_count + field // per_row
            lane = (field % per_row) * stride
            page_ref[row : row + 1, lane : lane + slot_count] = digit.astype(jnp.float32)
    for target in range(out_ref.shape[0]):
        out_ref[target] = page_ref[...].astype(out_ref.dtype)


def make_notes(tokens, slot_owner, slot_dest, seq_count):
    row_count, width = tokens.shape
    slot_count = slot_dest.shape[0]
    stride = -(-slot_count // LANES) * LANES
    used = row_count + -(-6 // (width // stride))
    rows = -(-used // CHUNK_ROWS) * CHUNK_ROWS
    vmem = pl.BlockSpec(memory_space=pltpu.VMEM)
    return pl.pallas_call(
        functools.partial(note_body, row_count, stride),
        out_shape=jax.ShapeDtypeStruct((seq_count, rows, width), tokens.dtype),
        in_specs=[vmem] * 3,
        out_specs=vmem,
        scratch_shapes=[pltpu.VMEM((rows, width), jnp.float32)],
        name="make_notes",
    )(tokens, slot_dest.reshape(1, -1), slot_owner.T)


def gather_notes(tokens, slot_owner, slot_dest, seq_count):
    inner = 1 << ((seq_count.bit_length() - 1) // 2)
    outer = seq_count // inner
    assert inner * outer == seq_count
    lines = [[o * inner + i for o in range(outer)] for i in range(inner)]
    planes = [[o * inner + i for i in range(inner)] for o in range(outer)]
    note = make_notes(tokens, slot_owner, slot_dest, outer)
    rows, width = note.shape[1:]
    along = lax.all_to_all(
        note, "seq", split_axis=0, concat_axis=0, axis_index_groups=lines, tiled=True
    )
    along = jnp.broadcast_to(along[None], (inner, outer, rows, width))
    across = lax.all_to_all(
        along, "seq", split_axis=0, concat_axis=0, axis_index_groups=planes, tiled=True
    )
    return jnp.swapaxes(across, 0, 1).reshape(seq_count, rows, width)


def read_notes(notes, row_count, slot_count):
    seq_count, rows, width = notes.shape
    stride = -(-slot_count // LANES) * LANES
    fields = notes[:, row_count:].reshape(seq_count, -1)[:, : 6 * stride]
    fields = fields.astype(jnp.float32).astype(jnp.int32).reshape(seq_count, 6, stride)
    fields = fields[:, :, :slot_count]
    return [fields[:, 2 * k] * 128 + fields[:, 2 * k + 1] - 1 for k in range(3)]


PACK_CUTS = 4


def wait_pages(group_ref, page_ref, group, total, sem):
    def many(i, carry):
        pltpu.make_async_copy(group_ref, group_ref, sem).wait()
        return carry

    def one(i, carry):
        pltpu.make_async_copy(page_ref, page_ref, sem).wait()
        return carry

    lax.fori_loop(0, total // group, many, 0)
    lax.fori_loop(0, total % group, one, 0)


def pack_body(
    slot_count, seq_count, capacity, dest_ref, pool_ref, out_ref, held_ref, count_ref, load_sem, send_sem
):
    scale = -(-(1 << QUOTIENT_SHIFT) // slot_count)
    last = seq_count * slot_count - 1
    assert last * (scale * slot_count - (1 << QUOTIENT_SHIFT)) < 1 << QUOTIENT_SHIFT
    assert last * scale < 1 << 31

    edges = [slot_count * cut // PACK_CUTS for cut in range(PACK_CUTS + 1)]
    loads = []
    for cut in range(PACK_CUTS):
        span = pl.ds(edges[cut], edges[cut + 1] - edges[cut])
        load = pltpu.make_async_copy(pool_ref.at[:, span], held_ref.at[:, span], load_sem.at[cut])
        load.start()
        loads.append(load)

    def reset(target, carry):
        count_ref[target] = 0
        return carry

    lax.fori_loop(0, seq_count, reset, 0)

    def send(slot, total):
        dest = dest_ref[slot]

        @pl.when(dest >= 0)
        def _():
            target = (dest * scale) >> QUOTIENT_SHIFT
            rank = count_ref[target]
            count_ref[target] = rank + 1
            pltpu.make_async_copy(
                held_ref.at[:, slot], out_ref.at[target, pl.ds(2 * rank, 2)], send_sem
            ).start()

        return total + (dest >= 0).astype(jnp.int32)

    total = 0
    for cut, load in enumerate(loads):
        load.wait()
        total = lax.fori_loop(edges[cut], edges[cut + 1], send, total)
    wait_pages(out_ref.at[0], out_ref.at[0, pl.ds(0, 2)], capacity, total, send_sem)


def pack_pages(kv_pool, slot_dest, seq_count, capacity):
    slot_count, page_size, width = kv_pool.shape[1:]
    block = (seq_count, 2 * capacity, page_size, width)
    hbm = pl.BlockSpec(memory_space=pltpu.HBM)
    return pl.pallas_call(
        functools.partial(pack_body, slot_count, seq_count, capacity),
        out_shape=jax.ShapeDtypeStruct(block, kv_pool.dtype),
        in_specs=[pl.BlockSpec(memory_space=pltpu.SMEM), hbm],
        out_specs=hbm,
        scratch_shapes=[
            pltpu.VMEM(kv_pool.shape, kv_pool.dtype),
            pltpu.SMEM((seq_count,), jnp.int32),
            pltpu.SemaphoreType.DMA((PACK_CUTS,)),
            pltpu.SemaphoreType.DMA,
        ],
        compiler_params=pltpu.CompilerParams(vmem_limit_bytes=MOST_VMEM),
        name="pack_pages",
    )(slot_dest, kv_pool)


def patched(page, fresh_ref, row_count, req, first):
    entry = lax.broadcasted_iota(jnp.int32, page.shape, 0)
    page = page.astype(jnp.float32)
    for step in range(STEPS):
        row = req * STEPS + step
        at = (row // row_count) * CHUNK_ROWS + row % row_count
        page = jnp.where(entry == first + step, fresh_ref[pl.ds(at, 1), :], page)
    return page.astype(jnp.bfloat16)


KEPT, BLANK, LANDED = 0, 1, 2


def keep_body(row_count, table_ref, pool_ref, key_ref, value_ref, out_ref, mark_ref):
    mark_ref[...] = jnp.zeros_like(mark_ref)

    def fill(slot, carry):
        kind = table_ref[0, slot]
        req = table_ref[2, slot]

        @pl.when(kind == KEPT)
        def _():
            out_ref[0, slot] = pool_ref[0, slot]
            out_ref[1, slot] = pool_ref[1, slot]

        @pl.when(kind == BLANK)
        def _():
            blank = jnp.zeros(out_ref.shape[2:], out_ref.dtype)
            out_ref[0, slot] = blank
            out_ref[1, slot] = blank

        @pl.when((req >= 0) & (kind == KEPT))
        def _():
            first = table_ref[3, slot]
            for which, fresh_ref in ((0, key_ref), (1, value_ref)):
                out_ref[which, slot] = patched(
                    out_ref[which, slot], fresh_ref, row_count, req, first
                )

        return carry

    lax.fori_loop(0, table_ref.shape[1], fill, 0)


MARK = jax.ShapeDtypeStruct((CHUNK_ROWS, LANES), jnp.float32)


def place_kept(row_count, table, kv_pool, key_new, value_new):
    vmem = pl.BlockSpec(memory_space=pltpu.VMEM)
    return pl.pallas_call(
        functools.partial(keep_body, row_count),
        out_shape=(jax.ShapeDtypeStruct(kv_pool.shape, kv_pool.dtype), MARK),
        in_specs=[pl.BlockSpec(memory_space=pltpu.SMEM)] + [vmem] * 3,
        out_specs=(vmem, vmem),
        compiler_params=pltpu.CompilerParams(vmem_limit_bytes=40 * 2**20),
        name="place_kept",
    )(table, kv_pool, key_new, value_new)


def land_body(
    row_count, capacity, table_ref, arrived_ref, key_ref, value_ref, begun_ref, out_ref, mark_ref,
    held_ref, stage_ref, load_sem, sem,
):
    load = pltpu.make_async_copy(arrived_ref, held_ref, load_sem)
    load.start()
    mark_ref[...] = jnp.zeros_like(mark_ref)
    load.wait()

    def send(slot, count):
        landed = table_ref[0, slot] == LANDED
        base = table_ref[1, slot]
        req = table_ref[2, slot]

        @pl.when(landed & (req < 0))
        def _():
            pltpu.make_async_copy(held_ref.at[pl.ds(base, 2)], out_ref.at[:, slot], sem).start()

        @pl.when(landed & (req >= 0))
        def _():
            first = table_ref[3, slot]
            for which, fresh_ref in ((0, key_ref), (1, value_ref)):
                stage_ref[slot, which] = patched(
                    held_ref[base + which], fresh_ref, row_count, req, first
                )
            pltpu.make_async_copy(stage_ref.at[slot], out_ref.at[:, slot], sem).start()

        return count + landed.astype(jnp.int32)

    count = lax.fori_loop(0, table_ref.shape[1], send, 0)
    wait_pages(stage_ref.at[pl.ds(0, capacity)], stage_ref.at[0], capacity, count, sem)


def place_landed(row_count, capacity, table, begun, arrived, key_new, value_new):
    slot_count, page_size, width = begun.shape[1:]
    vmem = pl.BlockSpec(memory_space=pltpu.VMEM)
    hbm = pl.BlockSpec(memory_space=pltpu.HBM)
    arrived = arrived.reshape(-1, page_size, width)
    return pl.pallas_call(
        functools.partial(land_body, row_count, capacity),
        out_shape=(jax.ShapeDtypeStruct(begun.shape, begun.dtype), MARK),
        in_specs=[pl.BlockSpec(memory_space=pltpu.SMEM), hbm, vmem, vmem, hbm],
        out_specs=(hbm, vmem),
        scratch_shapes=[
            pltpu.VMEM(arrived.shape, begun.dtype),
            pltpu.VMEM((slot_count, 2, page_size, width), begun.dtype),
            pltpu.SemaphoreType.DMA,
            pltpu.SemaphoreType.DMA,
        ],
        input_output_aliases={4: 0},
        compiler_params=pltpu.CompilerParams(vmem_limit_bytes=MOST_VMEM),
        name="place_landed",
    )(table, arrived, key_new, value_new, begun)


def split_parts(value):
    parts = []
    for _ in range(STAT_PARTS):
        part = value.astype(jnp.bfloat16).astype(jnp.float32)
        parts.append(part)
        value = value - part
    return parts


def attend_body(
    kv_count, group_size, seq_count, row_count,
    index_ref, mark_ref, query_ref, key_new_ref, value_new_ref, key_req_ref, pool_ref,
    out_ref, whole_ref,
):
    rows = query_ref.shape[0]
    width = kv_count * HD
    slot_count, page_size = pool_ref.shape[1:3]
    q_count = kv_count * group_size
    stack = rows * group_size
    row, held = row_ids(lax.broadcasted_iota(jnp.int32, (stack, 1), 0) % rows, row_count)
    row_req = jnp.where(held, row // STEPS, -2)
    new_row, new_held = row_ids(lax.broadcasted_iota(jnp.int32, (stack, rows), 1), row_count)
    mine = (row_req % seq_count) == index_ref[0]
    new_mask = (new_row // STEPS == row_req) & new_held & (new_row <= row) & mine
    stride = width // CHUNK_ROWS
    lane = lax.broadcasted_iota(jnp.int32, (rows, LANES), 1) % stride
    stats = jnp.zeros((rows, LANES), jnp.float32)
    for head in range(kv_count):
        cols = slice(head * HD, (head + 1) * HD)
        query = jnp.concatenate(
            [
                query_ref[:, (head * group_size + g) * HD : (head * group_size + g + 1) * HD]
                for g in range(group_size)
            ],
            axis=0,
        )
        contract = (((1,), (1,)), ((), ()))
        old_key = pool_ref[0, :, :, cols].reshape(slot_count * page_size, HD)
        old_value = pool_ref[1, :, :, cols].reshape(slot_count * page_size, HD)
        old = lax.dot_general(
            query, old_key, contract, preferred_element_type=jnp.float32
        ) * HD ** (-0.5)
        fresh = lax.dot_general(
            query, key_new_ref[:, cols], contract, preferred_element_type=jnp.float32
        ) * HD ** (-0.5)
        old_mask = key_req_ref[...] == row_req
        old = jnp.where(old_mask, old, NEG_FILL)
        fresh = jnp.where(new_mask, fresh, NEG_FILL)
        top = jnp.maximum(
            jnp.max(old, axis=1, keepdims=True), jnp.max(fresh, axis=1, keepdims=True)
        )
        old = jnp.where(old_mask, jnp.exp(old - top), 0.0)
        fresh = jnp.where(new_mask, jnp.exp(fresh - top), 0.0)
        total = jnp.sum(old, axis=1, keepdims=True) + jnp.sum(fresh, axis=1, keepdims=True)
        summed = jnp.dot(
            old.astype(jnp.bfloat16), old_value, preferred_element_type=jnp.float32
        ) + jnp.dot(
            fresh.astype(jnp.bfloat16), value_new_ref[:, cols], preferred_element_type=jnp.float32
        )
        summed = summed / jnp.where(total > 0.0, total, 1.0)
        parts = split_parts(top) + split_parts(total)
        for g in range(group_size):
            at = head * group_size + g
            own = slice(g * rows, (g + 1) * rows)
            whole_ref[:, at * HD : (at + 1) * HD] = summed[own]
            for k, part in enumerate(parts):
                stats = jnp.where(lane == k * q_count + at, part[own], stats)
    stats = jnp.concatenate([stats] * (width // LANES), axis=1)
    place = lax.broadcasted_iota(jnp.int32, (CHUNK_ROWS, width), 1) // stride
    chunk_row = lax.broadcasted_iota(jnp.int32, (CHUNK_ROWS, width), 0)
    for chunk in range(seq_count):
        span = slice(chunk * CHUNK_ROWS, (chunk + 1) * CHUNK_ROWS)
        line = jnp.sum(jnp.where(place == chunk_row, stats[span], 0.0), axis=0, keepdims=True)
        pieces = [whole_ref[span, g * width : (g + 1) * width] for g in range(group_size)]
        pieces[0] = jnp.where(chunk_row == row_count, line, pieces[0])
        out_ref[chunk] = jnp.concatenate(pieces, axis=0).astype(out_ref.dtype)


def attend(
    my_index, seq_count, row_count, mark, queries, key_new, value_new, key_req, kv_pool
):
    slot_count, page_size, width = kv_pool.shape[1:]
    kv_count = width // HD
    rows, q_width = queries.shape
    group_size = q_width // width
    assert group_size * CHUNK_ROWS == page_size and row_count < CHUNK_ROWS
    assert 2 * STAT_PARTS * kv_count * group_size <= width // CHUNK_ROWS
    smem = pl.BlockSpec(memory_space=pltpu.SMEM)
    vmem = pl.BlockSpec(memory_space=pltpu.VMEM)
    return pl.pallas_call(
        functools.partial(attend_body, kv_count, group_size, seq_count, row_count),
        out_shape=jax.ShapeDtypeStruct((seq_count, page_size, width), jnp.bfloat16),
        in_specs=[smem, pl.BlockSpec(memory_space=pl.ANY)] + [vmem] * 5,
        out_specs=vmem,
        scratch_shapes=[pltpu.VMEM((rows, q_width), jnp.float32)],
        compiler_params=pltpu.CompilerParams(vmem_limit_bytes=48 * 2**20),
        name="attend",
    )(
        my_index.reshape(1).astype(jnp.int32), mark, queries, key_new, value_new, key_req, kv_pool
    )


WEIGHT_CUTS = 4


def combine_body(q_count, row_count, mark_ref, part_ref, weight_ref, out_ref, held_ref, load_sem):
    depth = weight_ref.shape[0] // min(WEIGHT_CUTS, q_count)
    loads = []
    for cut in range(weight_ref.shape[0] // depth):
        span = pl.ds(cut * depth, depth)
        load = pltpu.make_async_copy(weight_ref.at[span], held_ref.at[span], load_sem.at[cut])
        load.start()
        loads.append(load)
    seq_count, page_size, width = part_ref.shape
    stride = width // CHUNK_ROWS
    place = lax.broadcasted_iota(jnp.int32, (CHUNK_ROWS, width), 1) // stride
    chunk_row = lax.broadcasted_iota(jnp.int32, (CHUNK_ROWS, width), 0)
    tops, sums = [], []
    for sender in range(seq_count):
        line = part_ref[sender, :CHUNK_ROWS, :].astype(jnp.float32)[row_count : row_count + 1]
        stats = jnp.where(place == chunk_row, line, 0.0)
        shift = width // 2
        while shift >= stride:
            stats = stats + pltpu.roll(stats, shift, 1)
            shift //= 2
        pieces = [stats[:, k * q_count : (k + 1) * q_count] for k in range(2 * STAT_PARTS)]
        tops.append(sum(pieces[1:STAT_PARTS], pieces[0]))
        sums.append(sum(pieces[STAT_PARTS + 1 :], pieces[STAT_PARTS]))
    peak = functools.reduce(jnp.maximum, tops)
    shares = [total * jnp.exp(top - peak) for top, total in zip(tops, sums)]
    whole = sum(shares[1:], shares[0])
    inverse = 1.0 / jnp.where(whole > 0.0, whole, 1.0)
    shares = [share * inverse for share in shares]
    attended = []
    for head in range(q_count):
        half = head * HD // width
        lane = head * HD - half * width
        acc = jnp.zeros((CHUNK_ROWS, HD), jnp.float32)
        for sender in range(seq_count):
            block = part_ref[sender, half * CHUNK_ROWS : (half + 1) * CHUNK_ROWS, lane : lane + HD]
            acc = acc + block.astype(jnp.float32) * shares[sender][:, head : head + 1]
        attended.append(acc.astype(jnp.bfloat16))
    attended = jnp.concatenate(attended, axis=1)
    total = jnp.zeros(out_ref.shape, jnp.float32)
    for cut, load in enumerate(loads):
        load.wait()
        span = slice(cut * depth, (cut + 1) * depth)
        total = total + jnp.dot(
            attended[:, span], held_ref[span, :], preferred_element_type=jnp.float32
        )
    out_ref[...] = total.astype(out_ref.dtype)


def combine(mark, arrived, w_out, row_count):
    vmem = pl.BlockSpec(memory_space=pltpu.VMEM)
    return pl.pallas_call(
        functools.partial(combine_body, w_out.shape[0] // HD, row_count),
        out_shape=jax.ShapeDtypeStruct((CHUNK_ROWS, w_out.shape[1]), jnp.bfloat16),
        in_specs=[
            pl.BlockSpec(memory_space=pl.ANY), vmem, pl.BlockSpec(memory_space=pltpu.HBM)
        ],
        out_specs=vmem,
        scratch_shapes=[
            pltpu.VMEM(w_out.shape, w_out.dtype),
            pltpu.SemaphoreType.DMA((WEIGHT_CUTS,)),
        ],
        compiler_params=pltpu.CompilerParams(vmem_limit_bytes=MOST_VMEM),
        name="combine",
    )(mark, arrived, w_out)


def length_of(lengths, request):
    hot = request[..., None] == jnp.arange(lengths.shape[0], dtype=jnp.int32)
    return jnp.sum(jnp.where(hot, lengths, 0), axis=-1)


def slot_table(notes, row_count, my_index, capacity, slot_owner, slot_dest, lengths, page_size):
    seq_count = notes.shape[0]
    slot_count = slot_dest.shape[0]
    dest, req, page = read_notes(notes, row_count, slot_count)
    sender = jnp.arange(seq_count, dtype=jnp.int32)[:, None]
    inner = dest - my_index * slot_count
    to_me = (inner >= 0) & (inner < slot_count)
    rank = jnp.cumsum(to_me.astype(jnp.int32), axis=1) - 1
    base = 2 * (sender * capacity + rank)
    match = inner.reshape(1, -1) == jnp.arange(slot_count, dtype=jnp.int32)[:, None]

    def pick(value):
        return jnp.sum(jnp.where(match, value.reshape(1, -1) + 1, 0), axis=1) - 1

    landed_base = pick(base)
    landed = landed_base >= 0
    stays = slot_dest < 0
    kind = jnp.where(landed, LANDED, jnp.where(stays, KEPT, BLANK))
    held_req = jnp.where(landed, pick(req), jnp.where(stays, slot_owner[:, 0], -1))
    held_page = jnp.where(landed, pick(page), slot_owner[:, 1])
    first = length_of(lengths, held_req) - held_page * page_size
    fresh = (held_req >= 0) & (first > -STEPS) & (first < page_size)
    return jnp.stack([kind, landed_base, jnp.where(fresh, held_req, -1), first])


def local(tokens, norm_gain, w_query, w_key_value, w_out, kv_pool, slot_owner, slot_dest, lengths):
    seq_count = lax.axis_size("seq")
    tp_count = lax.axis_size("tp")
    my_index = lax.axis_index("seq")
    row_count, token_width = tokens.shape
    slot_count, page_size = kv_pool.shape[1:3]
    capacity = -(-slot_count // seq_count)

    notes = gather_notes(tokens, slot_owner, slot_dest, seq_count)
    outgoing = pack_pages(kv_pool, slot_dest, seq_count, capacity)
    outgoing, notes = lax.optimization_barrier((outgoing, notes))
    arrived = lax.all_to_all(outgoing, "seq", split_axis=0, concat_axis=0, tiled=True)

    seq_tokens = notes[:, :CHUNK_ROWS].reshape(seq_count * CHUNK_ROWS, token_width)
    all_tokens = lax.all_gather(seq_tokens, "tp", axis=1, tiled=True)
    queries, key_new, value_new = project_rows(
        all_tokens, row_count, norm_gain, w_query, w_key_value, lengths
    )
    table = slot_table(
        notes, row_count, my_index, capacity, slot_owner, slot_dest, lengths, page_size
    )
    key_wide, value_wide = key_new.astype(jnp.float32), value_new.astype(jnp.float32)
    begun, mark = place_kept(row_count, table, kv_pool, key_wide, value_wide)
    owner_req = slot_owner[:, 0]
    base_len = length_of(lengths, owner_req)
    position = slot_owner[:, 1][:, None] * page_size + jnp.arange(page_size, dtype=jnp.int32)[None, :]
    key_req = jnp.where(position < base_len[:, None], owner_req[:, None], -1).reshape(1, -1)
    payload = attend(
        my_index, seq_count, row_count, mark, queries, key_new, value_new, key_req, kv_pool
    )
    payload, arrived = lax.optimization_barrier((payload, arrived))
    partials = lax.all_to_all(payload, "seq", split_axis=0, concat_axis=0, tiled=True)

    kv_moved, mark = place_landed(row_count, capacity, table, begun, arrived, key_wide, value_wide)
    partial_out = combine(mark, partials, w_out, row_count)[:row_count]
    if tp_count == 2:
        half = partial_out.shape[1] // 2
        swap = lax.axis_index("tp") == 0
        low, high = partial_out[:, :half], partial_out[:, half:]
        other = lax.ppermute(jnp.where(swap, high, low), "tp", [(0, 1), (1, 0)])
        own = jnp.where(swap, low, high)
        attn_out = (own.astype(jnp.float32) + other.astype(jnp.float32)).astype(jnp.bfloat16)
    else:
        attn_out = lax.psum_scatter(partial_out, "tp", scatter_dimension=1, tiled=True)
    return (attn_out, kv_moved)


def solution(mesh):
    in_specs = (
        P("seq", "tp"),
        P(),
        P(None, "tp"),
        P(None, None, "tp"),
        P("tp", None),
        P(None, "seq", None, "tp"),
        P("seq", None),
        P("seq"),
        P(),
    )
    out_specs = (P("seq", "tp"), P(None, "seq", None, "tp"))
    return jax.shard_map(local, mesh=mesh, in_specs=in_specs, out_specs=out_specs, check_vma=False)
```

```python
import functools

import jax
import jax.numpy as jnp
import numpy as np
from jax import lax
from jax.experimental import pallas as pl
from jax.experimental.pallas import tpu as pltpu
from jax.sharding import PartitionSpec as P

HD = 128
STEPS = 4
STAT_PARTS = 3
CHUNK_ROWS = 8
MOST_VMEM = 60 * 2**20
LANES = 128
QUOTIENT_SHIFT = 20

ROPE_BASE = 1000000.0
NEG_FILL = -1e30
NORM_EPS = 1e-06


def rotate(projected, positions, head_count):
    row_count = projected.shape[0]
    width = projected.shape[1] // head_count
    half_width = width // 2
    heads_view = projected.reshape(row_count, head_count, width)
    frequency = ROPE_BASE ** (-jnp.arange(half_width, dtype=jnp.float32) * 2.0 / width)
    angles = positions.astype(jnp.float32)[:, None] * frequency[None, :]
    cosine = jnp.cos(angles)[:, None, :]
    sine_part = jnp.sin(angles)[:, None, :]
    lower_half = heads_view[:, :, :half_width]
    upper_half = heads_view[:, :, half_width:]
    turned = jnp.concatenate(
        [
            lower_half * cosine - upper_half * sine_part,
            upper_half * cosine + lower_half * sine_part,
        ],
        axis=2,
    )
    return turned.reshape(row_count, head_count * width)


def row_ids(row, row_count):
    inner = row % CHUNK_ROWS
    return (row // CHUNK_ROWS) * row_count + inner, inner < row_count


def project_rows(token_block, row_count, norm_gain, w_query, w_key_value, lengths):
    row, held = row_ids(np.arange(token_block.shape[0], dtype=np.int32), row_count)
    row = np.where(held, row, 0)
    positions = length_of(lengths, jnp.asarray(row // STEPS)) + jnp.asarray(row % STEPS)
    widened = token_block.astype(jnp.float32)
    mean_square = jnp.mean(widened * widened, axis=1, keepdims=True)
    normed = (widened * lax.rsqrt(mean_square + NORM_EPS) * norm_gain[None, :]).astype(jnp.bfloat16)
    queries = jnp.dot(normed, w_query, preferred_element_type=jnp.float32)
    keyval = jnp.einsum("rd,cde->cre", normed, w_key_value, preferred_element_type=jnp.float32)
    queries = rotate(queries, positions, w_query.shape[1] // HD).astype(jnp.bfloat16)
    fresh_key = rotate(keyval[0], positions, w_key_value.shape[2] // HD).astype(jnp.bfloat16)
    fresh_value = keyval[1].astype(jnp.bfloat16)
    return queries, fresh_key, fresh_value


def note_body(row_count, stride, token_ref, dest_ref, owner_ref, out_ref, page_ref):
    width = token_ref.shape[1]
    slot_count = dest_ref.shape[1]
    page_ref[...] = jnp.zeros_like(page_ref)
    page_ref[:row_count, :] = token_ref[...].astype(jnp.float32)
    per_row = width // stride
    values = (dest_ref[...], owner_ref[0:1, :], owner_ref[1:2, :])
    for k, value in enumerate(values):
        for part, digit in enumerate(((value + 1) >> 7, (value + 1) & 127)):
            field = 2 * k + part
            row = row_count + field // per_row
            lane = (field % per_row) * stride
            page_ref[row : row + 1, lane : lane + slot_count] = digit.astype(jnp.float32)
    out_ref[...] = page_ref[...].astype(out_ref.dtype)


def make_note(tokens, slot_owner, slot_dest):
    row_count, width = tokens.shape
    slot_count = slot_dest.shape[0]
    stride = -(-slot_count // LANES) * LANES
    used = row_count + -(-6 // (width // stride))
    rows = -(-used // CHUNK_ROWS) * CHUNK_ROWS
    vmem = pl.BlockSpec(memory_space=pltpu.VMEM)
    return pl.pallas_call(
        functools.partial(note_body, row_count, stride),
        out_shape=jax.ShapeDtypeStruct((rows, width), tokens.dtype),
        in_specs=[vmem] * 3,
        out_specs=vmem,
        scratch_shapes=[pltpu.VMEM((rows, width), jnp.float32)],
        name="make_note",
    )(tokens, slot_dest.reshape(1, -1), slot_owner.T)


def sort_body(inner, index_ref, *refs):
    part_refs, out_ref = refs[:-1], refs[-1]
    near, far = index_ref[0] & (inner - 1), index_ref[0] // inner
    for shift, part_ref in enumerate(part_refs):
        for step in range(part_ref.shape[0]):
            out_ref[(far ^ step) * inner + (near ^ shift)] = part_ref[step]


def sort_notes(my_index, parts):
    inner = len(parts)
    far_count, rows, width = parts[0].shape
    vmem = pl.BlockSpec(memory_space=pltpu.VMEM)
    return pl.pallas_call(
        functools.partial(sort_body, inner),
        out_shape=jax.ShapeDtypeStruct((far_count * inner, rows, width), parts[0].dtype),
        in_specs=[pl.BlockSpec(memory_space=pltpu.SMEM)] + [vmem] * inner,
        out_specs=vmem,
        compiler_params=pltpu.CompilerParams(vmem_limit_bytes=16 * 2**20),
        name="sort_notes",
    )(my_index.reshape(1).astype(jnp.int32), *parts)


def read_notes(notes, row_count, slot_count):
    seq_count, rows, width = notes.shape
    stride = -(-slot_count // LANES) * LANES
    fields = notes[:, row_count:].reshape(seq_count, -1)[:, : 6 * stride]
    fields = fields.astype(jnp.float32).astype(jnp.int32).reshape(seq_count, 6, stride)
    fields = fields[:, :, :slot_count]
    return [fields[:, 2 * k] * 128 + fields[:, 2 * k + 1] - 1 for k in range(3)]


PACK_CUTS = 4


def wait_pages(group_ref, page_ref, group, total, sem):
    def many(i, carry):
        pltpu.make_async_copy(group_ref, group_ref, sem).wait()
        return carry

    def one(i, carry):
        pltpu.make_async_copy(page_ref, page_ref, sem).wait()
        return carry

    lax.fori_loop(0, total // group, many, 0)
    lax.fori_loop(0, total % group, one, 0)


def pack_body(
    slot_count, seq_count, capacity, dest_ref, pool_ref, out_ref, held_ref, count_ref, load_sem, send_sem
):
    scale = -(-(1 << QUOTIENT_SHIFT) // slot_count)
    last = seq_count * slot_count - 1
    assert last * (scale * slot_count - (1 << QUOTIENT_SHIFT)) < 1 << QUOTIENT_SHIFT
    assert last * scale < 1 << 31

    edges = [slot_count * cut // PACK_CUTS for cut in range(PACK_CUTS + 1)]
    loads = []
    for cut in range(PACK_CUTS):
        span = pl.ds(edges[cut], edges[cut + 1] - edges[cut])
        load = pltpu.make_async_copy(pool_ref.at[:, span], held_ref.at[:, span], load_sem.at[cut])
        load.start()
        loads.append(load)

    def reset(target, carry):
        count_ref[target] = 0
        return carry

    lax.fori_loop(0, seq_count, reset, 0)

    def send(slot, total):
        dest = dest_ref[slot]

        @pl.when(dest >= 0)
        def _():
            target = (dest * scale) >> QUOTIENT_SHIFT
            rank = count_ref[target]
            count_ref[target] = rank + 1
            pltpu.make_async_copy(
                held_ref.at[:, slot], out_ref.at[target, pl.ds(2 * rank, 2)], send_sem
            ).start()

        return total + (dest >= 0).astype(jnp.int32)

    total = 0
    for cut, load in enumerate(loads):
        load.wait()
        total = lax.fori_loop(edges[cut], edges[cut + 1], send, total)
    wait_pages(out_ref.at[0], out_ref.at[0, pl.ds(0, 2)], capacity, total, send_sem)


def pack_pages(kv_pool, slot_dest, seq_count, capacity):
    slot_count, page_size, width = kv_pool.shape[1:]
    block = (seq_count, 2 * capacity, page_size, width)
    hbm = pl.BlockSpec(memory_space=pltpu.HBM)
    return pl.pallas_call(
        functools.partial(pack_body, slot_count, seq_count, capacity),
        out_shape=jax.ShapeDtypeStruct(block, kv_pool.dtype),
        in_specs=[pl.BlockSpec(memory_space=pltpu.SMEM), hbm],
        out_specs=hbm,
        scratch_shapes=[
            pltpu.VMEM(kv_pool.shape, kv_pool.dtype),
            pltpu.SMEM((seq_count,), jnp.int32),
            pltpu.SemaphoreType.DMA((PACK_CUTS,)),
            pltpu.SemaphoreType.DMA,
        ],
        compiler_params=pltpu.CompilerParams(vmem_limit_bytes=MOST_VMEM),
        cost_estimate=moved(2 * kv_pool.size),
        name="pack_pages",
    )(slot_dest, kv_pool)


def patched(page, fresh_ref, row_count, req, first):
    entry = lax.broadcasted_iota(jnp.int32, page.shape, 0)
    page = page.astype(jnp.float32)
    for step in range(STEPS):
        row = req * STEPS + step
        at = (row // row_count) * CHUNK_ROWS + row % row_count
        page = jnp.where(entry == first + step, fresh_ref[pl.ds(at, 1), :], page)
    return page.astype(jnp.bfloat16)


KEPT, BLANK, LANDED = 0, 1, 2


def keep_body(row_count, table_ref, pool_ref, key_ref, value_ref, after_ref, out_ref, mark_ref):
    mark_ref[...] = jnp.zeros_like(mark_ref)

    def fill(slot, carry):
        kind = table_ref[0, slot]
        req = table_ref[1, slot]

        @pl.when(kind == KEPT)
        def _():
            out_ref[0, slot] = pool_ref[0, slot]
            out_ref[1, slot] = pool_ref[1, slot]

        @pl.when(kind == BLANK)
        def _():
            blank = jnp.zeros(out_ref.shape[2:], out_ref.dtype)
            out_ref[0, slot] = blank
            out_ref[1, slot] = blank

        @pl.when((req >= 0) & (kind == KEPT))
        def _():
            first = table_ref[2, slot]
            for which, fresh_ref in ((0, key_ref), (1, value_ref)):
                out_ref[which, slot] = patched(
                    out_ref[which, slot], fresh_ref, row_count, req, first
                )

        return carry

    lax.fori_loop(0, table_ref.shape[1], fill, 0)


def moved(elements, flops=0):
    return pl.CostEstimate(flops=flops, bytes_accessed=2 * elements, transcendentals=0)


MARK = jax.ShapeDtypeStruct((CHUNK_ROWS, LANES), jnp.float32)


def place_kept(row_count, table, kv_pool, key_new, value_new, after):
    vmem = pl.BlockSpec(memory_space=pltpu.VMEM)
    return pl.pallas_call(
        functools.partial(keep_body, row_count),
        out_shape=(jax.ShapeDtypeStruct(kv_pool.shape, kv_pool.dtype), MARK),
        in_specs=[pl.BlockSpec(memory_space=pltpu.SMEM)]
        + [vmem] * 3
        + [pl.BlockSpec(memory_space=pl.ANY)],
        out_specs=(vmem, vmem),
        compiler_params=pltpu.CompilerParams(vmem_limit_bytes=24 * 2**20),
        cost_estimate=moved(3 * kv_pool.size),
        name="place_kept",
    )(table, kv_pool, key_new, value_new, after)


def land_body(
    row_count, capacity, table_ref, held_ref, key_ref, value_ref, begun_ref, out_ref, mark_ref,
    stage_ref, sem,
):
    places = table_ref.shape[1]
    mark_ref[...] = jnp.zeros_like(mark_ref)

    def send(place, count):
        slot = table_ref[0, place]
        req = table_ref[1, place]

        @pl.when((slot >= 0) & (req < 0))
        def _():
            pltpu.make_async_copy(
                held_ref.at[pl.ds(2 * place, 2)], out_ref.at[:, slot], sem
            ).start()

        @pl.when((slot >= 0) & (req >= 0))
        def _():
            first = table_ref[2, place]
            for which, fresh_ref in ((0, key_ref), (1, value_ref)):
                stage_ref[slot, which] = patched(
                    held_ref[2 * place + which], fresh_ref, row_count, req, first
                )
            pltpu.make_async_copy(stage_ref.at[slot], out_ref.at[:, slot], sem).start()

        return count + (slot >= 0).astype(jnp.int32)

    count = lax.fori_loop(0, places, send, 0)
    wait_pages(stage_ref.at[pl.ds(0, capacity)], stage_ref.at[0], capacity, count, sem)


def place_landed(row_count, table, begun, arrived, key_new, value_new):
    slot_count, page_size, width = begun.shape[1:]
    capacity = arrived.shape[1] // 2
    vmem = pl.BlockSpec(memory_space=pltpu.VMEM)
    hbm = pl.BlockSpec(memory_space=pltpu.HBM)
    arrived = arrived.reshape(-1, page_size, width)
    return pl.pallas_call(
        functools.partial(land_body, row_count, capacity),
        out_shape=(jax.ShapeDtypeStruct(begun.shape, begun.dtype), MARK),
        in_specs=[pl.BlockSpec(memory_space=pltpu.SMEM), vmem, vmem, vmem, hbm],
        out_specs=(hbm, vmem),
        scratch_shapes=[
            pltpu.VMEM((slot_count, 2, page_size, width), begun.dtype),
            pltpu.SemaphoreType.DMA,
        ],
        input_output_aliases={4: 0},
        compiler_params=pltpu.CompilerParams(vmem_limit_bytes=32 * 2**20),
        cost_estimate=moved(3 * begun.size),
        name="place_landed",
    )(table, pltpu.with_memory_space_constraint(arrived, pltpu.VMEM), key_new, value_new, begun)


def split_parts(value):
    parts = []
    for _ in range(STAT_PARTS):
        part = value.astype(jnp.bfloat16).astype(jnp.float32)
        parts.append(part)
        value = value - part
    return parts


def attend_body(
    kv_count, group_size, seq_count, row_count,
    index_ref, query_ref, key_new_ref, value_new_ref, key_req_ref, pool_ref, *rest,
):
    out_refs, whole_ref, chunk_ref = rest[:-2], rest[-2], rest[-1]
    rows = query_ref.shape[0]
    width = kv_count * HD
    slot_count, page_size = pool_ref.shape[1:3]
    q_count = kv_count * group_size
    stack = rows * group_size
    row, held = row_ids(lax.broadcasted_iota(jnp.int32, (stack, 1), 0) % rows, row_count)
    row_req = jnp.where(held, row // STEPS, -2)
    new_row, new_held = row_ids(lax.broadcasted_iota(jnp.int32, (stack, rows), 1), row_count)
    mine = (row_req % seq_count) == index_ref[0]
    new_mask = (new_row // STEPS == row_req) & new_held & (new_row <= row) & mine
    stride = width // CHUNK_ROWS
    lane = lax.broadcasted_iota(jnp.int32, (rows, LANES), 1) % stride
    stats = jnp.zeros((rows, LANES), jnp.float32)
    for head in range(kv_count):
        cols = slice(head * HD, (head + 1) * HD)
        query = jnp.concatenate(
            [
                query_ref[:, (head * group_size + g) * HD : (head * group_size + g + 1) * HD]
                for g in range(group_size)
            ],
            axis=0,
        )
        contract = (((1,), (1,)), ((), ()))
        old_key = pool_ref[0, :, :, cols].reshape(slot_count * page_size, HD)
        old_value = pool_ref[1, :, :, cols].reshape(slot_count * page_size, HD)
        old = lax.dot_general(
            query, old_key, contract, preferred_element_type=jnp.float32
        ) * HD ** (-0.5)
        fresh = lax.dot_general(
            query, key_new_ref[:, cols], contract, preferred_element_type=jnp.float32
        ) * HD ** (-0.5)
        old_mask = key_req_ref[...] == row_req
        old = jnp.where(old_mask, old, NEG_FILL)
        fresh = jnp.where(new_mask, fresh, NEG_FILL)
        top = jnp.maximum(
            jnp.max(old, axis=1, keepdims=True), jnp.max(fresh, axis=1, keepdims=True)
        )
        old = jnp.where(old_mask, jnp.exp(old - top), 0.0)
        fresh = jnp.where(new_mask, jnp.exp(fresh - top), 0.0)
        total = jnp.sum(old, axis=1, keepdims=True) + jnp.sum(fresh, axis=1, keepdims=True)
        summed = jnp.dot(
            old.astype(jnp.bfloat16), old_value, preferred_element_type=jnp.float32
        ) + jnp.dot(
            fresh.astype(jnp.bfloat16), value_new_ref[:, cols], preferred_element_type=jnp.float32
        )
        summed = summed / jnp.where(total > 0.0, total, 1.0)
        parts = split_parts(top) + split_parts(total)
        for g in range(group_size):
            at = head * group_size + g
            own = slice(g * rows, (g + 1) * rows)
            whole_ref[:, at * HD : (at + 1) * HD] = summed[own]
            for k, part in enumerate(parts):
                stats = jnp.where(lane == k * q_count + at, part[own], stats)
    stats = jnp.concatenate([stats] * (width // LANES), axis=1)
    place = lax.broadcasted_iota(jnp.int32, (CHUNK_ROWS, width), 1) // stride
    chunk_row = lax.broadcasted_iota(jnp.int32, (CHUNK_ROWS, width), 0)
    for chunk in range(seq_count):
        span = slice(chunk * CHUNK_ROWS, (chunk + 1) * CHUNK_ROWS)
        line = jnp.sum(jnp.where(place == chunk_row, stats[span], 0.0), axis=0, keepdims=True)
        pieces = [whole_ref[span, g * width : (g + 1) * width] for g in range(group_size)]
        pieces[0] = jnp.where(chunk_row == row_count, line, pieces[0])
        chunk_ref[chunk] = jnp.concatenate(pieces, axis=0).astype(chunk_ref.dtype)
    inner = len(out_refs)
    own = index_ref[0] & (inner - 1)
    for shift, out_ref in enumerate(out_refs):
        for far in range(seq_count // inner):
            out_ref[far] = chunk_ref[far * inner + (own ^ shift)]


def attend(
    my_index, seq_count, inner, row_count, queries, key_new, value_new, key_req, kv_pool
):
    slot_count, page_size, width = kv_pool.shape[1:]
    kv_count = width // HD
    rows, q_width = queries.shape
    group_size = q_width // width
    assert group_size * CHUNK_ROWS == page_size and row_count < CHUNK_ROWS
    assert 2 * STAT_PARTS * kv_count * group_size <= width // CHUNK_ROWS
    smem = pl.BlockSpec(memory_space=pltpu.SMEM)
    vmem = pl.BlockSpec(memory_space=pltpu.VMEM)
    return pl.pallas_call(
        functools.partial(attend_body, kv_count, group_size, seq_count, row_count),
        out_shape=(jax.ShapeDtypeStruct((seq_count // inner, page_size, width), jnp.bfloat16),)
        * inner,
        in_specs=[smem] + [vmem] * 5,
        out_specs=(vmem,) * inner,
        scratch_shapes=[
            pltpu.VMEM((rows, q_width), jnp.float32),
            pltpu.VMEM((seq_count, page_size, width), jnp.bfloat16),
        ],
        compiler_params=pltpu.CompilerParams(vmem_limit_bytes=36 * 2**20),
        cost_estimate=moved(2 * kv_pool.size, 4 * rows * q_width * slot_count * page_size),
        name="attend",
    )(
        my_index.reshape(1).astype(jnp.int32), queries, key_new, value_new, key_req, kv_pool
    )


def merge_units(units, q_count, row_count):
    width = units[0].shape[1]
    stride = width // CHUNK_ROWS
    place = lax.broadcasted_iota(jnp.int32, (CHUNK_ROWS, width), 1) // stride
    chunk_row = lax.broadcasted_iota(jnp.int32, (CHUNK_ROWS, width), 0)
    tops, sums = [], []
    for unit in units:
        stats = jnp.where(place == chunk_row, unit[row_count : row_count + 1], 0.0)
        shift = width // 2
        while shift >= stride:
            stats = stats + pltpu.roll(stats, shift, 1)
            shift //= 2
        stats = stats[:, :LANES]
        pieces = [stats] + [
            pltpu.roll(stats, LANES - k * q_count, 1) for k in range(1, 2 * STAT_PARTS)
        ]
        tops.append(sum(pieces[1:STAT_PARTS], pieces[0]))
        sums.append(sum(pieces[STAT_PARTS + 1 :], pieces[STAT_PARTS]))
    lane = lax.broadcasted_iota(jnp.int32, (CHUNK_ROWS, LANES), 1)
    tops = [jnp.where(lane < q_count, top, 0.0) for top in tops]
    sums = [jnp.where(lane < q_count, total, 0.0) for total in sums]
    peak = functools.reduce(jnp.maximum, tops)
    shares = [total * jnp.exp(top - peak) for top, total in zip(tops, sums)]
    whole = sum(shares[1:], shares[0])
    inverse = 1.0 / jnp.where(whole > 0.0, whole, 1.0)
    shares = [share * inverse for share in shares]
    heads = []
    for head in range(q_count):
        half = head * HD // width
        at = head * HD - half * width
        acc = jnp.zeros((CHUNK_ROWS, HD), jnp.float32)
        for unit, share in zip(units, shares):
            block = unit[half * CHUNK_ROWS : (half + 1) * CHUNK_ROWS, at : at + HD]
            acc = acc + block * share[:, head : head + 1]
        heads.append(acc)
    return heads, peak, whole


def merge_body(q_count, row_count, index_ref, mark_ref, weight_ref, *rest):
    rest, near_ref, held_ref, load_sem = rest[:-3], rest[-3], rest[-2], rest[-1]
    load = pltpu.make_async_copy(weight_ref, near_ref, load_sem)
    load.start()
    far_count = rest[0].shape[0]
    part_refs, out_refs = rest[:-far_count], rest[-far_count:]
    width = held_ref.shape[2]
    stride = width // CHUNK_ROWS
    place = lax.broadcasted_iota(jnp.int32, (CHUNK_ROWS, width), 1) // stride
    chunk_row = lax.broadcasted_iota(jnp.int32, (CHUNK_ROWS, width), 0)
    for far in range(far_count):
        units = [part_ref[far].astype(jnp.float32) for part_ref in part_refs]
        heads, peak, whole = merge_units(units, q_count, row_count)
        stats = jnp.zeros((CHUNK_ROWS, LANES), jnp.float32)
        for k, part in enumerate(split_parts(peak) + split_parts(whole)):
            stats = stats + (pltpu.roll(part, k * q_count, 1) if k else part)
        shift = stride
        while shift < LANES:
            stats = stats + pltpu.roll(stats, shift, 1)
            shift *= 2
        stats = jnp.concatenate([stats] * (width // LANES), axis=1)
        line = jnp.sum(jnp.where(place == chunk_row, stats, 0.0), axis=0, keepdims=True)
        numerators = jnp.concatenate(heads, axis=1)
        pieces = [
            numerators[:, g * width : (g + 1) * width]
            for g in range(numerators.shape[1] // width)
        ]
        pieces[0] = jnp.where(chunk_row == row_count, line, pieces[0])
        held_ref[far] = jnp.concatenate(pieces, axis=0).astype(held_ref.dtype)
    own = index_ref[0] // len(part_refs)
    for shift, out_ref in enumerate(out_refs):
        out_ref[...] = held_ref[own ^ shift]
    load.wait()


def merge(my_index, mark, w_out, parts, q_count, row_count):
    far_count, page_size, width = parts[0].shape
    vmem = pl.BlockSpec(memory_space=pltpu.VMEM)
    unit = jax.ShapeDtypeStruct((page_size, width), jnp.bfloat16)
    return pl.pallas_call(
        functools.partial(merge_body, q_count, row_count),
        out_shape=(unit,) * far_count + (pltpu.VMEM(w_out.shape, w_out.dtype),),
        in_specs=[
            pl.BlockSpec(memory_space=pltpu.SMEM),
            pl.BlockSpec(memory_space=pl.ANY),
            pl.BlockSpec(memory_space=pltpu.HBM),
        ]
        + [vmem] * len(parts),
        out_specs=(vmem,) * (far_count + 1),
        scratch_shapes=[
            pltpu.VMEM((far_count, page_size, width), jnp.bfloat16),
            pltpu.SemaphoreType.DMA,
        ],
        compiler_params=pltpu.CompilerParams(vmem_limit_bytes=24 * 2**20),
        cost_estimate=moved(3 * 2**20),
        name="merge",
    )(my_index.reshape(1).astype(jnp.int32), mark, w_out, *parts)


def combine_body(q_count, row_count, tp_count, index_ref, *refs):
    part_refs, weight_ref, out_refs = refs[: -1 - tp_count], refs[-1 - tp_count], refs[-tp_count:]
    units = [part_ref[...].astype(jnp.float32) for part_ref in part_refs]
    heads, _, _ = merge_units(units, q_count, row_count)
    attended = jnp.concatenate([head.astype(jnp.bfloat16) for head in heads], axis=1)
    total = jnp.dot(attended, weight_ref[...], preferred_element_type=jnp.float32)
    width = total.shape[1] // tp_count
    blocks = [total[:, k * width : (k + 1) * width] for k in range(tp_count)]
    for shift, out_ref in enumerate(out_refs):
        chosen = blocks[0]
        for k in range(1, tp_count):
            chosen = jnp.where((index_ref[0] ^ shift) == k, blocks[k], chosen)
        out_ref[...] = chosen.astype(out_ref.dtype)


def combine(tp_index, tp_count, parts, w_near, row_count):
    vmem = pl.BlockSpec(memory_space=pltpu.VMEM)
    block = jax.ShapeDtypeStruct((CHUNK_ROWS, w_near.shape[1] // tp_count), jnp.bfloat16)
    return pl.pallas_call(
        functools.partial(combine_body, w_near.shape[0] // HD, row_count, tp_count),
        out_shape=(block,) * tp_count,
        in_specs=[pl.BlockSpec(memory_space=pltpu.SMEM)] + [vmem] * (len(parts) + 1),
        out_specs=(vmem,) * tp_count,
        compiler_params=pltpu.CompilerParams(vmem_limit_bytes=24 * 2**20),
        cost_estimate=moved(2 * w_near.size),
        name="combine",
    )(tp_index.reshape(1).astype(jnp.int32), *parts, w_near)


def close_body(mark_ref, *refs):
    part_refs, out_ref = refs[:-1], refs[-1]
    total = part_refs[0][...].astype(jnp.float32)
    for part_ref in part_refs[1:]:
        total = total + part_ref[...].astype(jnp.float32)
    out_ref[...] = total[: out_ref.shape[0]].astype(out_ref.dtype)


def close(mark, parts, row_count):
    vmem = pl.BlockSpec(memory_space=pltpu.VMEM)
    return pl.pallas_call(
        close_body,
        out_shape=jax.ShapeDtypeStruct((row_count, parts[0].shape[1]), jnp.bfloat16),
        in_specs=[pl.BlockSpec(memory_space=pl.ANY)] + [vmem] * len(parts),
        out_specs=vmem,
        compiler_params=pltpu.CompilerParams(vmem_limit_bytes=16 * 2**20),
        name="close",
    )(mark, *parts)


def swap_all(parts, step, count, axis="seq"):
    pairs = [[(i, i ^ (k * step)) for i in range(count)] for k in range(len(parts))]
    return [parts[0]] + [lax.ppermute(parts[k], axis, pairs[k]) for k in range(1, len(parts))]


def length_of(lengths, request):
    hot = request[..., None] == jnp.arange(lengths.shape[0], dtype=jnp.int32)
    return jnp.sum(jnp.where(hot, lengths, 0), axis=-1)


def slot_tables(notes, row_count, my_index, capacity, slot_owner, slot_dest, lengths, page_size):
    seq_count = notes.shape[0]
    slot_count = slot_dest.shape[0]
    dest, req, page = read_notes(notes, row_count, slot_count)
    inner = dest - my_index * slot_count
    to_me = (inner >= 0) & (inner < slot_count)
    rank = jnp.cumsum(to_me.astype(jnp.int32), axis=1) - 1
    match = to_me[:, None, :] & (
        rank[:, None, :] == jnp.arange(capacity, dtype=jnp.int32)[None, :, None]
    )

    def pick(value):
        return jnp.sum(jnp.where(match, value[:, None, :] + 1, 0), axis=2).reshape(-1) - 1

    def fresh(request, held_page):
        first = length_of(lengths, request) - held_page * page_size
        hit = (request >= 0) & (first > -STEPS) & (first < page_size)
        return jnp.where(hit, request, -1), first

    slot = pick(inner)
    by_place = jnp.stack([slot, *fresh(pick(req), pick(page))])
    landed = jnp.any(slot[None, :] == jnp.arange(slot_count, dtype=jnp.int32)[:, None], axis=1)
    stays = slot_dest < 0
    kind = jnp.where(landed, LANDED, jnp.where(stays, KEPT, BLANK))
    held_req = jnp.where(kind == KEPT, slot_owner[:, 0], -1)
    by_slot = jnp.stack([kind, *fresh(held_req, slot_owner[:, 1])])
    return by_slot, by_place


def local(tokens, norm_gain, w_query, w_key_value, w_out, kv_pool, slot_owner, slot_dest, lengths):
    seq_count = lax.axis_size("seq")
    tp_count = lax.axis_size("tp")
    my_index = lax.axis_index("seq")
    row_count, token_width = tokens.shape
    slot_count, page_size = kv_pool.shape[1:3]
    capacity = -(-slot_count // seq_count)

    inner = 1 << ((seq_count.bit_length() - 1) // 2)
    note = make_note(tokens, slot_owner, slot_dest)
    along = swap_all([note] * (seq_count // inner), inner, seq_count)
    outgoing = pack_pages(kv_pool, slot_dest, seq_count, capacity)
    outgoing, along, lengths = lax.optimization_barrier((outgoing, along, lengths))
    notes = sort_notes(my_index, swap_all([jnp.stack(along)] * inner, 1, seq_count))
    arrived = lax.all_to_all(outgoing, "seq", split_axis=0, concat_axis=0, tiled=True)

    seq_tokens = notes[:, :CHUNK_ROWS].reshape(seq_count * CHUNK_ROWS, token_width)
    all_tokens = lax.all_gather(seq_tokens, "tp", axis=1, tiled=True)
    queries, key_new, value_new = project_rows(
        all_tokens, row_count, norm_gain, w_query, w_key_value, lengths
    )
    by_slot, by_place = slot_tables(
        notes, row_count, my_index, capacity, slot_owner, slot_dest, lengths, page_size
    )
    key_wide, value_wide = key_new.astype(jnp.float32), value_new.astype(jnp.float32)
    owner_req = slot_owner[:, 0]
    base_len = length_of(lengths, owner_req)
    position = slot_owner[:, 1][:, None] * page_size + jnp.arange(page_size, dtype=jnp.int32)[None, :]
    key_req = jnp.where(position < base_len[:, None], owner_req[:, None], -1).reshape(1, -1)
    payload = attend(
        my_index, seq_count, inner, row_count, queries, key_new, value_new, key_req, kv_pool
    )
    begun, mark = place_kept(row_count, by_slot, kv_pool, key_wide, value_wide, payload[0])
    near = swap_all(payload, 1, seq_count)
    *merged, w_near = merge(my_index, mark, w_out, near, w_query.shape[1] // HD, row_count)
    far = swap_all(merged, inner, seq_count)
    columns = combine(lax.axis_index("tp"), tp_count, far, w_near, row_count)
    columns = swap_all(columns, 1, tp_count, "tp")
    kv_moved, mark = place_landed(row_count, by_place, begun, arrived, key_wide, value_wide)
    attn_out = close(mark, columns, row_count)
    return (attn_out, kv_moved)


def solution(mesh):
    in_specs = (
        P("seq", "tp"),
        P(),
        P(None, "tp"),
        P(None, None, "tp"),
        P("tp", None),
        P(None, "seq", None, "tp"),
        P("seq", None),
        P("seq"),
        P(),
    )
    out_specs = (P("seq", "tp"), P(None, "seq", None, "tp"))
    return jax.shard_map(local, mesh=mesh, in_specs=in_specs, out_specs=out_specs, check_vma=False)
```

```python
import functools

import jax
import jax.numpy as jnp
import numpy as np
from jax import lax
from jax.experimental import pallas as pl
from jax.experimental.pallas import tpu as pltpu
from jax.sharding import PartitionSpec as P

HD = 128
STEPS = 4
STAT_PARTS = 3
CHUNK_ROWS = 8
MOST_VMEM = 60 * 2**20
LANES = 128
QUOTIENT_SHIFT = 20

ROPE_BASE = 1000000.0
NEG_FILL = -1e30
NORM_EPS = 1e-06


def rotate(projected, positions, head_count):
    row_count = projected.shape[0]
    width = projected.shape[1] // head_count
    half_width = width // 2
    heads_view = projected.reshape(row_count, head_count, width)
    frequency = ROPE_BASE ** (-jnp.arange(half_width, dtype=jnp.float32) * 2.0 / width)
    angles = positions.astype(jnp.float32)[:, None] * frequency[None, :]
    cosine = jnp.cos(angles)[:, None, :]
    sine_part = jnp.sin(angles)[:, None, :]
    lower_half = heads_view[:, :, :half_width]
    upper_half = heads_view[:, :, half_width:]
    turned = jnp.concatenate(
        [
            lower_half * cosine - upper_half * sine_part,
            upper_half * cosine + lower_half * sine_part,
        ],
        axis=2,
    )
    return turned.reshape(row_count, head_count * width)


def row_ids(row, row_count):
    inner = row % CHUNK_ROWS
    return (row // CHUNK_ROWS) * row_count + inner, inner < row_count


def project_rows(token_block, row_count, norm_gain, w_query, w_key_value, lengths):
    row, held = row_ids(np.arange(token_block.shape[0], dtype=np.int32), row_count)
    row = np.where(held, row, 0)
    positions = length_of(lengths, jnp.asarray(row // STEPS)) + jnp.asarray(row % STEPS)
    widened = token_block.astype(jnp.float32)
    mean_square = jnp.mean(widened * widened, axis=1, keepdims=True)
    normed = (widened * lax.rsqrt(mean_square + NORM_EPS) * norm_gain[None, :]).astype(jnp.bfloat16)
    queries = jnp.dot(normed, w_query, preferred_element_type=jnp.float32)
    keyval = jnp.einsum("rd,cde->cre", normed, w_key_value, preferred_element_type=jnp.float32)
    queries = rotate(queries, positions, w_query.shape[1] // HD).astype(jnp.bfloat16)
    fresh_key = rotate(keyval[0], positions, w_key_value.shape[2] // HD).astype(jnp.bfloat16)
    fresh_value = keyval[1].astype(jnp.bfloat16)
    return queries, fresh_key, fresh_value


def note_body(row_count, stride, token_ref, dest_ref, owner_ref, out_ref, page_ref):
    width = token_ref.shape[1]
    slot_count = dest_ref.shape[1]
    page_ref[...] = jnp.zeros_like(page_ref)
    page_ref[:row_count, :] = token_ref[...].astype(jnp.float32)
    per_row = width // stride
    values = (dest_ref[...], owner_ref[0:1, :], owner_ref[1:2, :])
    for k, value in enumerate(values):
        for part, digit in enumerate(((value + 1) >> 7, (value + 1) & 127)):
            field = 2 * k + part
            row = row_count + field // per_row
            lane = (field % per_row) * stride
            page_ref[row : row + 1, lane : lane + slot_count] = digit.astype(jnp.float32)
    out_ref[...] = page_ref[...].astype(out_ref.dtype)


def make_note(tokens, slot_owner, slot_dest):
    row_count, width = tokens.shape
    slot_count = slot_dest.shape[0]
    stride = -(-slot_count // LANES) * LANES
    used = row_count + -(-6 // (width // stride))
    rows = -(-used // CHUNK_ROWS) * CHUNK_ROWS
    vmem = pl.BlockSpec(memory_space=pltpu.VMEM)
    return pl.pallas_call(
        functools.partial(note_body, row_count, stride),
        out_shape=jax.ShapeDtypeStruct((rows, width), tokens.dtype),
        in_specs=[vmem] * 3,
        out_specs=vmem,
        scratch_shapes=[pltpu.VMEM((rows, width), jnp.float32)],
        name="make_note",
    )(tokens, slot_dest.reshape(1, -1), slot_owner.T)


def sort_body(inner, index_ref, *refs):
    part_refs, out_ref = refs[:-1], refs[-1]
    near, far = index_ref[0] & (inner - 1), index_ref[0] // inner
    for shift, part_ref in enumerate(part_refs):
        for step in range(part_ref.shape[0]):
            out_ref[(far ^ step) * inner + (near ^ shift)] = part_ref[step]


def sort_notes(my_place, parts):
    inner = len(parts)
    far_count, rows, width = parts[0].shape
    vmem = pl.BlockSpec(memory_space=pltpu.VMEM)
    return pl.pallas_call(
        functools.partial(sort_body, inner),
        out_shape=jax.ShapeDtypeStruct((far_count * inner, rows, width), parts[0].dtype),
        in_specs=[pl.BlockSpec(memory_space=pltpu.SMEM)] + [vmem] * inner,
        out_specs=vmem,
        compiler_params=pltpu.CompilerParams(vmem_limit_bytes=16 * 2**20),
        name="sort_notes",
    )(my_place, *parts)


def read_notes(notes, row_count, slot_count):
    seq_count, rows, width = notes.shape
    stride = -(-slot_count // LANES) * LANES
    fields = notes[:, row_count:].reshape(seq_count, -1)[:, : 6 * stride]
    fields = fields.astype(jnp.float32).astype(jnp.int32).reshape(seq_count, 6, stride)
    fields = fields[:, :, :slot_count]
    return [fields[:, 2 * k] * 128 + fields[:, 2 * k + 1] - 1 for k in range(3)]


PACK_CUTS = 4


def wait_pages(group_ref, page_ref, group, total, sem):
    def many(i, carry):
        pltpu.make_async_copy(group_ref, group_ref, sem).wait()
        return carry

    def one(i, carry):
        pltpu.make_async_copy(page_ref, page_ref, sem).wait()
        return carry

    lax.fori_loop(0, total // group, many, 0)
    lax.fori_loop(0, total % group, one, 0)


def pack_body(
    slot_count, seq_count, capacity, dest_ref, pool_ref, out_ref, held_ref, count_ref, load_sem, send_sem
):
    scale = -(-(1 << QUOTIENT_SHIFT) // slot_count)
    last = seq_count * slot_count - 1
    assert last * (scale * slot_count - (1 << QUOTIENT_SHIFT)) < 1 << QUOTIENT_SHIFT
    assert last * scale < 1 << 31

    edges = [slot_count * cut // PACK_CUTS for cut in range(PACK_CUTS + 1)]
    loads = []
    for cut in range(PACK_CUTS):
        span = pl.ds(edges[cut], edges[cut + 1] - edges[cut])
        load = pltpu.make_async_copy(pool_ref.at[:, span], held_ref.at[:, span], load_sem.at[cut])
        load.start()
        loads.append(load)

    def reset(target, carry):
        count_ref[target] = 0
        return carry

    lax.fori_loop(0, seq_count, reset, 0)

    def send(slot, total):
        dest = dest_ref[slot]

        @pl.when(dest >= 0)
        def _():
            target = (dest * scale) >> QUOTIENT_SHIFT
            rank = count_ref[target]
            count_ref[target] = rank + 1
            pltpu.make_async_copy(
                held_ref.at[:, slot], out_ref.at[target, pl.ds(2 * rank, 2)], send_sem
            ).start()

        return total + (dest >= 0).astype(jnp.int32)

    total = 0
    for cut, load in enumerate(loads):
        load.wait()
        total = lax.fori_loop(edges[cut], edges[cut + 1], send, total)
    wait_pages(out_ref.at[0], out_ref.at[0, pl.ds(0, 2)], capacity, total, send_sem)


def pack_pages(kv_pool, slot_dest, seq_count, capacity):
    slot_count, page_size, width = kv_pool.shape[1:]
    block = (seq_count, 2 * capacity, page_size, width)
    hbm = pl.BlockSpec(memory_space=pltpu.HBM)
    return pl.pallas_call(
        functools.partial(pack_body, slot_count, seq_count, capacity),
        out_shape=jax.ShapeDtypeStruct(block, kv_pool.dtype),
        in_specs=[pl.BlockSpec(memory_space=pltpu.SMEM), hbm],
        out_specs=hbm,
        scratch_shapes=[
            pltpu.VMEM(kv_pool.shape, kv_pool.dtype),
            pltpu.SMEM((seq_count,), jnp.int32),
            pltpu.SemaphoreType.DMA((PACK_CUTS,)),
            pltpu.SemaphoreType.DMA,
        ],
        compiler_params=pltpu.CompilerParams(vmem_limit_bytes=MOST_VMEM),
        cost_estimate=moved(2 * kv_pool.size),
        name="pack_pages",
    )(slot_dest, kv_pool)


def patched(page, fresh_ref, row_count, req, first):
    entry = lax.broadcasted_iota(jnp.int32, page.shape, 0)
    page = page.astype(jnp.float32)
    for step in range(STEPS):
        row = req * STEPS + step
        at = (row // row_count) * CHUNK_ROWS + row % row_count
        page = jnp.where(entry == first + step, fresh_ref[pl.ds(at, 1), :], page)
    return page.astype(jnp.bfloat16)


KEPT, BLANK, LANDED = 0, 1, 2


def keep_body(row_count, table_ref, pool_ref, key_ref, value_ref, after_ref, ready_ref, out_ref, mark_ref):
    mark_ref[...] = jnp.zeros_like(mark_ref)

    def fill(slot, carry):
        kind = table_ref[0, slot]
        req = table_ref[1, slot]

        @pl.when(kind == KEPT)
        def _():
            out_ref[0, slot] = pool_ref[0, slot]
            out_ref[1, slot] = pool_ref[1, slot]

        @pl.when(kind == BLANK)
        def _():
            blank = jnp.zeros(out_ref.shape[2:], out_ref.dtype)
            out_ref[0, slot] = blank
            out_ref[1, slot] = blank

        @pl.when((req >= 0) & (kind == KEPT))
        def _():
            first = table_ref[2, slot]
            for which, fresh_ref in ((0, key_ref), (1, value_ref)):
                out_ref[which, slot] = patched(
                    out_ref[which, slot], fresh_ref, row_count, req, first
                )

        return carry

    lax.fori_loop(0, table_ref.shape[1], fill, 0)


def moved(elements, flops=0):
    return pl.CostEstimate(flops=flops, bytes_accessed=2 * elements, transcendentals=0)


MARK = jax.ShapeDtypeStruct((CHUNK_ROWS, LANES), jnp.float32)


def place_kept(row_count, table, kv_pool, key_new, value_new, after, ready):
    vmem = pl.BlockSpec(memory_space=pltpu.VMEM)
    return pl.pallas_call(
        functools.partial(keep_body, row_count),
        out_shape=(jax.ShapeDtypeStruct(kv_pool.shape, kv_pool.dtype), MARK),
        in_specs=[pl.BlockSpec(memory_space=pltpu.SMEM)]
        + [vmem] * 3
        + [pl.BlockSpec(memory_space=pl.ANY)] * 2,
        out_specs=(vmem, vmem),
        compiler_params=pltpu.CompilerParams(vmem_limit_bytes=24 * 2**20),
        cost_estimate=moved(3 * kv_pool.size),
        name="place_kept",
    )(table, kv_pool, key_new, value_new, after, ready)


LAND_CUTS = 7


def land_body(
    row_count, capacity, table_ref, arrived_ref, key_ref, value_ref, begun_ref, out_ref, mark_ref,
    held_ref, load_sem, sem,
):
    places = table_ref.shape[1]
    edges = [places * cut // LAND_CUTS for cut in range(LAND_CUTS + 1)]
    loads = []
    for cut in range(LAND_CUTS):
        span = pl.ds(2 * edges[cut], 2 * (edges[cut + 1] - edges[cut]))
        load = pltpu.make_async_copy(arrived_ref.at[span], held_ref.at[span], load_sem.at[cut])
        load.start()
        loads.append(load)
    mark_ref[...] = jnp.zeros_like(mark_ref)

    def send(place, count):
        slot = table_ref[0, place]
        req = table_ref[1, place]

        @pl.when(slot >= 0)
        def _():
            @pl.when(req >= 0)
            def _():
                first = table_ref[2, place]
                for which, fresh_ref in ((0, key_ref), (1, value_ref)):
                    held_ref[2 * place + which] = patched(
                        held_ref[2 * place + which], fresh_ref, row_count, req, first
                    )

            pltpu.make_async_copy(
                held_ref.at[pl.ds(2 * place, 2)], out_ref.at[:, slot], sem
            ).start()

        return count + (slot >= 0).astype(jnp.int32)

    count = 0
    for cut, load in enumerate(loads):
        load.wait()
        count = lax.fori_loop(edges[cut], edges[cut + 1], send, count)
    group = held_ref.at[pl.ds(0, 2 * capacity)]
    wait_pages(group, held_ref.at[pl.ds(0, 2)], capacity, count, sem)


def place_landed(row_count, table, begun, arrived, key_new, value_new):
    slot_count, page_size, width = begun.shape[1:]
    capacity = arrived.shape[1] // 2
    vmem = pl.BlockSpec(memory_space=pltpu.VMEM)
    hbm = pl.BlockSpec(memory_space=pltpu.HBM)
    arrived = arrived.reshape(-1, page_size, width)
    return pl.pallas_call(
        functools.partial(land_body, row_count, capacity),
        out_shape=(jax.ShapeDtypeStruct(begun.shape, begun.dtype), MARK),
        in_specs=[pl.BlockSpec(memory_space=pltpu.SMEM), hbm, vmem, vmem, hbm],
        out_specs=(hbm, vmem),
        scratch_shapes=[
            pltpu.VMEM(arrived.shape, begun.dtype),
            pltpu.SemaphoreType.DMA((LAND_CUTS,)),
            pltpu.SemaphoreType.DMA,
        ],
        input_output_aliases={4: 0},
        compiler_params=pltpu.CompilerParams(vmem_limit_bytes=32 * 2**20),
        cost_estimate=moved(3 * begun.size),
        name="place_landed",
    )(table, arrived, key_new, value_new, begun)


def split_parts(value):
    parts = []
    for _ in range(STAT_PARTS):
        part = value.astype(jnp.bfloat16).astype(jnp.float32)
        parts.append(part)
        value = value - part
    return parts


def attend_body(
    kv_count, group_size, seq_count, row_count,
    index_ref, query_ref, key_new_ref, value_new_ref, key_req_ref, pool_ref, *rest,
):
    out_refs, whole_ref, chunk_ref = rest[:-2], rest[-2], rest[-1]
    rows = query_ref.shape[0]
    width = kv_count * HD
    slot_count, page_size = pool_ref.shape[1:3]
    q_count = kv_count * group_size
    stack = rows * group_size
    row, held = row_ids(lax.broadcasted_iota(jnp.int32, (stack, 1), 0) % rows, row_count)
    row_req = jnp.where(held, row // STEPS, -2)
    new_row, new_held = row_ids(lax.broadcasted_iota(jnp.int32, (stack, rows), 1), row_count)
    mine = (row_req % seq_count) == index_ref[0]
    new_mask = (new_row // STEPS == row_req) & new_held & (new_row <= row) & mine
    stride = width // CHUNK_ROWS
    lane = lax.broadcasted_iota(jnp.int32, (rows, LANES), 1) % stride
    stats = jnp.zeros((rows, LANES), jnp.float32)
    for head in range(kv_count):
        cols = slice(head * HD, (head + 1) * HD)
        query = jnp.concatenate(
            [
                query_ref[:, (head * group_size + g) * HD : (head * group_size + g + 1) * HD]
                for g in range(group_size)
            ],
            axis=0,
        )
        contract = (((1,), (1,)), ((), ()))
        old_key = pool_ref[0, :, :, cols].reshape(slot_count * page_size, HD)
        old_value = pool_ref[1, :, :, cols].reshape(slot_count * page_size, HD)
        old = lax.dot_general(
            query, old_key, contract, preferred_element_type=jnp.float32
        ) * HD ** (-0.5)
        fresh = lax.dot_general(
            query, key_new_ref[:, cols], contract, preferred_element_type=jnp.float32
        ) * HD ** (-0.5)
        old_mask = key_req_ref[...] == row_req
        old = jnp.where(old_mask, old, NEG_FILL)
        fresh = jnp.where(new_mask, fresh, NEG_FILL)
        top = jnp.maximum(
            jnp.max(old, axis=1, keepdims=True), jnp.max(fresh, axis=1, keepdims=True)
        )
        old = jnp.where(old_mask, jnp.exp(old - top), 0.0)
        fresh = jnp.where(new_mask, jnp.exp(fresh - top), 0.0)
        total = jnp.sum(old, axis=1, keepdims=True) + jnp.sum(fresh, axis=1, keepdims=True)
        summed = jnp.dot(
            old.astype(jnp.bfloat16), old_value, preferred_element_type=jnp.float32
        ) + jnp.dot(
            fresh.astype(jnp.bfloat16), value_new_ref[:, cols], preferred_element_type=jnp.float32
        )
        summed = summed / jnp.where(total > 0.0, total, 1.0)
        parts = split_parts(top) + split_parts(total)
        for g in range(group_size):
            at = head * group_size + g
            own = slice(g * rows, (g + 1) * rows)
            whole_ref[:, at * HD : (at + 1) * HD] = summed[own]
            for k, part in enumerate(parts):
                stats = jnp.where(lane == k * q_count + at, part[own], stats)
    stats = jnp.concatenate([stats] * (width // LANES), axis=1)
    place = lax.broadcasted_iota(jnp.int32, (CHUNK_ROWS, width), 1) // stride
    chunk_row = lax.broadcasted_iota(jnp.int32, (CHUNK_ROWS, width), 0)
    for chunk in range(seq_count):
        span = slice(chunk * CHUNK_ROWS, (chunk + 1) * CHUNK_ROWS)
        line = jnp.sum(jnp.where(place == chunk_row, stats[span], 0.0), axis=0, keepdims=True)
        pieces = [whole_ref[span, g * width : (g + 1) * width] for g in range(group_size)]
        pieces[0] = jnp.where(chunk_row == row_count, line, pieces[0])
        chunk_ref[chunk] = jnp.concatenate(pieces, axis=0).astype(chunk_ref.dtype)
    inner = len(out_refs)
    own = index_ref[0] & (inner - 1)
    for shift, out_ref in enumerate(out_refs):
        for far in range(seq_count // inner):
            out_ref[far] = chunk_ref[far * inner + (own ^ shift)]


def attend(
    my_place, seq_count, inner, row_count, queries, key_new, value_new, key_req, kv_pool
):
    slot_count, page_size, width = kv_pool.shape[1:]
    kv_count = width // HD
    rows, q_width = queries.shape
    group_size = q_width // width
    assert group_size * CHUNK_ROWS == page_size and row_count < CHUNK_ROWS
    assert 2 * STAT_PARTS * kv_count * group_size <= width // CHUNK_ROWS
    smem = pl.BlockSpec(memory_space=pltpu.SMEM)
    vmem = pl.BlockSpec(memory_space=pltpu.VMEM)
    return pl.pallas_call(
        functools.partial(attend_body, kv_count, group_size, seq_count, row_count),
        out_shape=(jax.ShapeDtypeStruct((seq_count // inner, page_size, width), jnp.bfloat16),)
        * inner,
        in_specs=[smem] + [vmem] * 5,
        out_specs=(vmem,) * inner,
        scratch_shapes=[
            pltpu.VMEM((rows, q_width), jnp.float32),
            pltpu.VMEM((seq_count, page_size, width), jnp.bfloat16),
        ],
        compiler_params=pltpu.CompilerParams(vmem_limit_bytes=48 * 2**20),
        cost_estimate=moved(2 * kv_pool.size, 4 * rows * q_width * slot_count * page_size),
        name="attend",
    )(
        my_place, queries, key_new, value_new, key_req, kv_pool
    )


def merge_units(units, q_count, row_count):
    width = units[0].shape[1]
    stride = width // CHUNK_ROWS
    place = lax.broadcasted_iota(jnp.int32, (CHUNK_ROWS, width), 1) // stride
    chunk_row = lax.broadcasted_iota(jnp.int32, (CHUNK_ROWS, width), 0)
    tops, sums = [], []
    for unit in units:
        stats = jnp.where(place == chunk_row, unit[row_count : row_count + 1], 0.0)
        shift = width // 2
        while shift >= stride:
            stats = stats + pltpu.roll(stats, shift, 1)
            shift //= 2
        stats = stats[:, :LANES]
        pieces = [stats] + [
            pltpu.roll(stats, LANES - k * q_count, 1) for k in range(1, 2 * STAT_PARTS)
        ]
        tops.append(sum(pieces[1:STAT_PARTS], pieces[0]))
        sums.append(sum(pieces[STAT_PARTS + 1 :], pieces[STAT_PARTS]))
    lane = lax.broadcasted_iota(jnp.int32, (CHUNK_ROWS, LANES), 1)
    tops = [jnp.where(lane < q_count, top, 0.0) for top in tops]
    sums = [jnp.where(lane < q_count, total, 0.0) for total in sums]
    peak = functools.reduce(jnp.maximum, tops)
    shares = [total * jnp.exp(top - peak) for top, total in zip(tops, sums)]
    whole = sum(shares[1:], shares[0])
    inverse = 1.0 / jnp.where(whole > 0.0, whole, 1.0)
    shares = [share * inverse for share in shares]
    heads = []
    for head in range(q_count):
        half = head * HD // width
        at = head * HD - half * width
        acc = jnp.zeros((CHUNK_ROWS, HD), jnp.float32)
        for unit, share in zip(units, shares):
            block = unit[half * CHUNK_ROWS : (half + 1) * CHUNK_ROWS, at : at + HD]
            acc = acc + block * share[:, head : head + 1]
        heads.append(acc)
    return heads, peak, whole


def merge_body(q_count, row_count, index_ref, mark_ref, weight_ref, *rest):
    rest, near_ref, held_ref, load_sem = rest[:-3], rest[-3], rest[-2], rest[-1]
    load = pltpu.make_async_copy(weight_ref, near_ref, load_sem)
    load.start()
    far_count = rest[0].shape[0]
    part_refs, out_refs = rest[:-far_count], rest[-far_count:]
    width = held_ref.shape[2]
    stride = width // CHUNK_ROWS
    place = lax.broadcasted_iota(jnp.int32, (CHUNK_ROWS, width), 1) // stride
    chunk_row = lax.broadcasted_iota(jnp.int32, (CHUNK_ROWS, width), 0)
    for far in range(far_count):
        units = [part_ref[far].astype(jnp.float32) for part_ref in part_refs]
        heads, peak, whole = merge_units(units, q_count, row_count)
        stats = jnp.zeros((CHUNK_ROWS, LANES), jnp.float32)
        for k, part in enumerate(split_parts(peak) + split_parts(whole)):
            stats = stats + (pltpu.roll(part, k * q_count, 1) if k else part)
        shift = stride
        while shift < LANES:
            stats = stats + pltpu.roll(stats, shift, 1)
            shift *= 2
        stats = jnp.concatenate([stats] * (width // LANES), axis=1)
        line = jnp.sum(jnp.where(place == chunk_row, stats, 0.0), axis=0, keepdims=True)
        numerators = jnp.concatenate(heads, axis=1)
        pieces = [
            numerators[:, g * width : (g + 1) * width]
            for g in range(numerators.shape[1] // width)
        ]
        pieces[0] = jnp.where(chunk_row == row_count, line, pieces[0])
        held_ref[far] = jnp.concatenate(pieces, axis=0).astype(held_ref.dtype)
    own = index_ref[0] // len(part_refs)
    for shift, out_ref in enumerate(out_refs):
        out_ref[...] = held_ref[own ^ shift]
    load.wait()


def merge(my_place, mark, w_out, parts, q_count, row_count):
    far_count, page_size, width = parts[0].shape
    vmem = pl.BlockSpec(memory_space=pltpu.VMEM)
    unit = jax.ShapeDtypeStruct((page_size, width), jnp.bfloat16)
    return pl.pallas_call(
        functools.partial(merge_body, q_count, row_count),
        out_shape=(unit,) * far_count + (pltpu.VMEM(w_out.shape, w_out.dtype),),
        in_specs=[
            pl.BlockSpec(memory_space=pltpu.SMEM),
            pl.BlockSpec(memory_space=pl.ANY),
            pl.BlockSpec(memory_space=pltpu.HBM),
        ]
        + [vmem] * len(parts),
        out_specs=(vmem,) * (far_count + 1),
        scratch_shapes=[
            pltpu.VMEM((far_count, page_size, width), jnp.bfloat16),
            pltpu.SemaphoreType.DMA,
        ],
        compiler_params=pltpu.CompilerParams(vmem_limit_bytes=24 * 2**20),
        cost_estimate=moved(3 * 2**20),
        name="merge",
    )(my_place, mark, w_out, *parts)


def combine_body(q_count, row_count, tp_count, index_ref, *refs):
    part_refs, weight_ref, out_refs = refs[: -1 - tp_count], refs[-1 - tp_count], refs[-tp_count:]
    units = [part_ref[...].astype(jnp.float32) for part_ref in part_refs]
    heads, _, _ = merge_units(units, q_count, row_count)
    attended = jnp.concatenate([head.astype(jnp.bfloat16) for head in heads], axis=1)
    total = jnp.dot(attended, weight_ref[...], preferred_element_type=jnp.float32)
    width = total.shape[1] // tp_count
    blocks = [total[:, k * width : (k + 1) * width] for k in range(tp_count)]
    for shift, out_ref in enumerate(out_refs):
        chosen = blocks[0]
        for k in range(1, tp_count):
            chosen = jnp.where((index_ref[1] ^ shift) == k, blocks[k], chosen)
        out_ref[...] = chosen.astype(out_ref.dtype)


def combine(my_place, tp_count, parts, w_near, row_count):
    vmem = pl.BlockSpec(memory_space=pltpu.VMEM)
    block = jax.ShapeDtypeStruct((CHUNK_ROWS, w_near.shape[1] // tp_count), jnp.bfloat16)
    return pl.pallas_call(
        functools.partial(combine_body, w_near.shape[0] // HD, row_count, tp_count),
        out_shape=(block,) * tp_count,
        in_specs=[pl.BlockSpec(memory_space=pltpu.SMEM)] + [vmem] * (len(parts) + 1),
        out_specs=(vmem,) * tp_count,
        compiler_params=pltpu.CompilerParams(vmem_limit_bytes=24 * 2**20),
        cost_estimate=moved(2 * w_near.size),
        name="combine",
    )(my_place, *parts, w_near)


def close_body(mark_ref, *refs):
    part_refs, out_ref = refs[:-1], refs[-1]
    total = part_refs[0][...].astype(jnp.float32)
    for part_ref in part_refs[1:]:
        total = total + part_ref[...].astype(jnp.float32)
    out_ref[...] = total[: out_ref.shape[0]].astype(out_ref.dtype)


def close(mark, parts, row_count):
    vmem = pl.BlockSpec(memory_space=pltpu.VMEM)
    return pl.pallas_call(
        close_body,
        out_shape=jax.ShapeDtypeStruct((row_count, parts[0].shape[1]), jnp.bfloat16),
        in_specs=[pl.BlockSpec(memory_space=pl.ANY)] + [vmem] * len(parts),
        out_specs=vmem,
        compiler_params=pltpu.CompilerParams(vmem_limit_bytes=16 * 2**20),
        name="close",
    )(mark, *parts)


def swap_all(parts, step, count, axis="seq"):
    pairs = [[(i, i ^ (k * step)) for i in range(count)] for k in range(len(parts))]
    return [parts[0]] + [lax.ppermute(parts[k], axis, pairs[k]) for k in range(1, len(parts))]


def length_of(lengths, request):
    hot = request[..., None] == jnp.arange(lengths.shape[0], dtype=jnp.int32)
    return jnp.sum(jnp.where(hot, lengths, 0), axis=-1)


def slot_tables(notes, row_count, my_index, capacity, slot_owner, slot_dest, lengths, page_size):
    seq_count = notes.shape[0]
    slot_count = slot_dest.shape[0]
    dest, req, page = read_notes(notes, row_count, slot_count)
    inner = dest - my_index * slot_count
    to_me = (inner >= 0) & (inner < slot_count)
    rank = jnp.cumsum(to_me.astype(jnp.int32), axis=1) - 1
    match = to_me[:, None, :] & (
        rank[:, None, :] == jnp.arange(capacity, dtype=jnp.int32)[None, :, None]
    )

    def pick(value):
        return jnp.sum(jnp.where(match, value[:, None, :] + 1, 0), axis=2).reshape(-1) - 1

    def fresh(request, held_page):
        first = length_of(lengths, request) - held_page * page_size
        hit = (request >= 0) & (first > -STEPS) & (first < page_size)
        return jnp.where(hit, request, -1), first

    slot = pick(inner)
    by_place = jnp.stack([slot, *fresh(pick(req), pick(page))])
    landed = jnp.any(slot[None, :] == jnp.arange(slot_count, dtype=jnp.int32)[:, None], axis=1)
    stays = slot_dest < 0
    kind = jnp.where(landed, LANDED, jnp.where(stays, KEPT, BLANK))
    held_req = jnp.where(kind == KEPT, slot_owner[:, 0], -1)
    by_slot = jnp.stack([kind, *fresh(held_req, slot_owner[:, 1])])
    return by_slot, by_place


def local(tokens, norm_gain, w_query, w_key_value, w_out, kv_pool, slot_owner, slot_dest, lengths):
    seq_count = lax.axis_size("seq")
    tp_count = lax.axis_size("tp")
    my_index = lax.axis_index("seq")
    my_place = jnp.stack([my_index, lax.axis_index("tp")]).astype(jnp.int32)
    row_count, token_width = tokens.shape
    slot_count, page_size = kv_pool.shape[1:3]
    capacity = -(-slot_count // seq_count)

    inner = 1 << ((seq_count.bit_length() - 1) // 2)
    note = make_note(tokens, slot_owner, slot_dest)
    along = swap_all([note] * (seq_count // inner), inner, seq_count)
    outgoing = pack_pages(kv_pool, slot_dest, seq_count, capacity)
    outgoing, along, lengths = lax.optimization_barrier((outgoing, along, lengths))
    notes = sort_notes(my_place, swap_all([jnp.stack(along)] * inner, 1, seq_count))
    arrived = lax.all_to_all(outgoing, "seq", split_axis=0, concat_axis=0, tiled=True)

    seq_tokens = notes[:, :CHUNK_ROWS].reshape(seq_count * CHUNK_ROWS, token_width)
    all_tokens = lax.all_gather(seq_tokens, "tp", axis=1, tiled=True)
    queries, key_new, value_new = project_rows(
        all_tokens, row_count, norm_gain, w_query, w_key_value, lengths
    )
    by_slot, by_place = slot_tables(
        notes, row_count, my_index, capacity, slot_owner, slot_dest, lengths, page_size
    )
    key_wide, value_wide = key_new.astype(jnp.float32), value_new.astype(jnp.float32)
    owner_req = slot_owner[:, 0]
    base_len = length_of(lengths, owner_req)
    position = slot_owner[:, 1][:, None] * page_size + jnp.arange(page_size, dtype=jnp.int32)[None, :]
    key_req = jnp.where(position < base_len[:, None], owner_req[:, None], -1).reshape(1, -1)
    payload = attend(
        my_place, seq_count, inner, row_count, queries, key_new, value_new, key_req, kv_pool
    )
    begun, mark = place_kept(row_count, by_slot, kv_pool, key_wide, value_wide, payload[0], by_place)
    near = swap_all(payload, 1, seq_count)
    *merged, w_near = merge(my_place, mark, w_out, near, w_query.shape[1] // HD, row_count)
    far = swap_all(merged, inner, seq_count)
    columns = combine(my_place, tp_count, far, w_near, row_count)
    columns = swap_all(columns, 1, tp_count, "tp")
    kv_moved, mark = place_landed(row_count, by_place, begun, arrived, key_wide, value_wide)
    attn_out = close(mark, columns, row_count)
    return (attn_out, kv_moved)


def solution(mesh):
    in_specs = (
        P("seq", "tp"),
        P(),
        P(None, "tp"),
        P(None, None, "tp"),
        P("tp", None),
        P(None, "seq", None, "tp"),
        P("seq", None),
        P("seq"),
        P(),
    )
    out_specs = (P("seq", "tp"), P(None, "seq", None, "tp"))
    return jax.shard_map(local, mesh=mesh, in_specs=in_specs, out_specs=out_specs, check_vma=False)
```

```python
import functools

import jax
import jax.numpy as jnp
import numpy as np
from jax import lax
from jax.experimental import pallas as pl
from jax.experimental.pallas import tpu as pltpu
from jax.sharding import PartitionSpec as P

HD = 128
STEPS = 4
STAT_PARTS = 3
CHUNK_ROWS = 8
MOST_VMEM = 60 * 2**20
LANES = 128
QUOTIENT_SHIFT = 20

ROPE_BASE = 1000000.0
NEG_FILL = -1e30
NORM_EPS = 1e-06


def rotate(projected, positions, head_count):
    row_count = projected.shape[0]
    width = projected.shape[1] // head_count
    half_width = width // 2
    heads_view = projected.reshape(row_count, head_count, width)
    frequency = ROPE_BASE ** (-jnp.arange(half_width, dtype=jnp.float32) * 2.0 / width)
    angles = positions.astype(jnp.float32)[:, None] * frequency[None, :]
    cosine = jnp.cos(angles)[:, None, :]
    sine_part = jnp.sin(angles)[:, None, :]
    lower_half = heads_view[:, :, :half_width]
    upper_half = heads_view[:, :, half_width:]
    turned = jnp.concatenate(
        [
            lower_half * cosine - upper_half * sine_part,
            upper_half * cosine + lower_half * sine_part,
        ],
        axis=2,
    )
    return turned.reshape(row_count, head_count * width)


def row_ids(row, row_count):
    inner = row % CHUNK_ROWS
    return (row // CHUNK_ROWS) * row_count + inner, inner < row_count


def project_rows(token_block, row_count, norm_gain, w_query, w_key_value, lengths):
    row, held = row_ids(np.arange(token_block.shape[0], dtype=np.int32), row_count)
    row = np.where(held, row, 0)
    positions = length_of(lengths, jnp.asarray(row // STEPS)) + jnp.asarray(row % STEPS)
    widened = token_block.astype(jnp.float32)
    mean_square = jnp.mean(widened * widened, axis=1, keepdims=True)
    normed = (widened * lax.rsqrt(mean_square + NORM_EPS) * norm_gain[None, :]).astype(jnp.bfloat16)
    queries = jnp.dot(normed, w_query, preferred_element_type=jnp.float32)
    keyval = jnp.einsum("rd,cde->cre", normed, w_key_value, preferred_element_type=jnp.float32)
    queries = rotate(queries, positions, w_query.shape[1] // HD).astype(jnp.bfloat16)
    fresh_key = rotate(keyval[0], positions, w_key_value.shape[2] // HD).astype(jnp.bfloat16)
    fresh_value = keyval[1].astype(jnp.bfloat16)
    return queries, fresh_key, fresh_value


def note_body(row_count, stride, token_ref, dest_ref, owner_ref, out_ref, page_ref):
    width = token_ref.shape[1]
    slot_count = dest_ref.shape[1]
    page_ref[...] = jnp.zeros_like(page_ref)
    page_ref[:row_count, :] = token_ref[...].astype(jnp.float32)
    per_row = width // stride
    values = (dest_ref[...], owner_ref[0:1, :], owner_ref[1:2, :])
    for k, value in enumerate(values):
        for part, digit in enumerate(((value + 1) >> 7, (value + 1) & 127)):
            field = 2 * k + part
            row = row_count + field // per_row
            lane = (field % per_row) * stride
            page_ref[row : row + 1, lane : lane + slot_count] = digit.astype(jnp.float32)
    out_ref[...] = page_ref[...].astype(out_ref.dtype)


def make_note(tokens, slot_owner, slot_dest):
    row_count, width = tokens.shape
    slot_count = slot_dest.shape[0]
    stride = -(-slot_count // LANES) * LANES
    used = row_count + -(-6 // (width // stride))
    rows = -(-used // CHUNK_ROWS) * CHUNK_ROWS
    vmem = pl.BlockSpec(memory_space=pltpu.VMEM)
    return pl.pallas_call(
        functools.partial(note_body, row_count, stride),
        out_shape=jax.ShapeDtypeStruct((rows, width), tokens.dtype),
        in_specs=[vmem] * 3,
        out_specs=vmem,
        scratch_shapes=[pltpu.VMEM((rows, width), jnp.float32)],
        name="make_note",
    )(tokens, slot_dest.reshape(1, -1), slot_owner.T)


def sort_body(inner, index_ref, *refs):
    part_refs, out_ref = refs[:-1], refs[-1]
    near, far = index_ref[0] & (inner - 1), index_ref[0] // inner
    for shift, part_ref in enumerate(part_refs):
        for step in range(part_ref.shape[0]):
            out_ref[(far ^ step) * inner + (near ^ shift)] = part_ref[step]


def sort_notes(my_place, parts):
    inner = len(parts)
    far_count, rows, width = parts[0].shape
    vmem = pl.BlockSpec(memory_space=pltpu.VMEM)
    return pl.pallas_call(
        functools.partial(sort_body, inner),
        out_shape=jax.ShapeDtypeStruct((far_count * inner, rows, width), parts[0].dtype),
        in_specs=[pl.BlockSpec(memory_space=pltpu.SMEM)] + [vmem] * inner,
        out_specs=vmem,
        compiler_params=pltpu.CompilerParams(vmem_limit_bytes=16 * 2**20),
        name="sort_notes",
    )(my_place, *parts)


def read_notes(notes, row_count, slot_count):
    seq_count, rows, width = notes.shape
    stride = -(-slot_count // LANES) * LANES
    fields = notes[:, row_count:].reshape(seq_count, -1)[:, : 6 * stride]
    fields = fields.astype(jnp.float32).astype(jnp.int32).reshape(seq_count, 6, stride)
    fields = fields[:, :, :slot_count]
    return [fields[:, 2 * k] * 128 + fields[:, 2 * k + 1] - 1 for k in range(3)]


PACK_CUTS = 4


def wait_pages(group_ref, page_ref, group, total, sem):
    def many(i, carry):
        pltpu.make_async_copy(group_ref, group_ref, sem).wait()
        return carry

    def one(i, carry):
        pltpu.make_async_copy(page_ref, page_ref, sem).wait()
        return carry

    lax.fori_loop(0, total // group, many, 0)
    lax.fori_loop(0, total % group, one, 0)


def pack_body(
    slot_count, seq_count, capacity, dest_ref, pool_ref, out_ref, held_ref, count_ref, load_sem, send_sem
):
    scale = -(-(1 << QUOTIENT_SHIFT) // slot_count)
    last = seq_count * slot_count - 1
    assert last * (scale * slot_count - (1 << QUOTIENT_SHIFT)) < 1 << QUOTIENT_SHIFT
    assert last * scale < 1 << 31

    edges = [slot_count * cut // PACK_CUTS for cut in range(PACK_CUTS + 1)]
    loads = []
    for cut in range(PACK_CUTS):
        span = pl.ds(edges[cut], edges[cut + 1] - edges[cut])
        load = pltpu.make_async_copy(pool_ref.at[:, span], held_ref.at[:, span], load_sem.at[cut])
        load.start()
        loads.append(load)

    def reset(target, carry):
        count_ref[target] = 0
        return carry

    lax.fori_loop(0, seq_count, reset, 0)

    def send(slot, total):
        dest = dest_ref[slot]

        @pl.when(dest >= 0)
        def _():
            target = (dest * scale) >> QUOTIENT_SHIFT
            rank = count_ref[target]
            count_ref[target] = rank + 1
            pltpu.make_async_copy(
                held_ref.at[:, slot], out_ref.at[target, pl.ds(2 * rank, 2)], send_sem
            ).start()

        return total + (dest >= 0).astype(jnp.int32)

    total = 0
    for cut, load in enumerate(loads):
        load.wait()
        total = lax.fori_loop(edges[cut], edges[cut + 1], send, total, unroll=4)
    wait_pages(out_ref.at[0], out_ref.at[0, pl.ds(0, 2)], capacity, total, send_sem)


def pack_pages(kv_pool, slot_dest, seq_count, capacity):
    slot_count, page_size, width = kv_pool.shape[1:]
    block = (seq_count, 2 * capacity, page_size, width)
    hbm = pl.BlockSpec(memory_space=pltpu.HBM)
    return pl.pallas_call(
        functools.partial(pack_body, slot_count, seq_count, capacity),
        out_shape=jax.ShapeDtypeStruct(block, kv_pool.dtype),
        in_specs=[pl.BlockSpec(memory_space=pltpu.SMEM), hbm],
        out_specs=hbm,
        scratch_shapes=[
            pltpu.VMEM(kv_pool.shape, kv_pool.dtype),
            pltpu.SMEM((seq_count,), jnp.int32),
            pltpu.SemaphoreType.DMA((PACK_CUTS,)),
            pltpu.SemaphoreType.DMA,
        ],
        compiler_params=pltpu.CompilerParams(vmem_limit_bytes=MOST_VMEM),
        cost_estimate=moved(2 * kv_pool.size),
        name="pack_pages",
    )(slot_dest, kv_pool)


def patched(page, fresh_ref, row_count, req, first):
    entry = lax.broadcasted_iota(jnp.int32, page.shape, 0)
    page = page.astype(jnp.float32)
    for step in range(STEPS):
        row = req * STEPS + step
        at = (row // row_count) * CHUNK_ROWS + row % row_count
        page = jnp.where(entry == first + step, fresh_ref[pl.ds(at, 1), :], page)
    return page.astype(jnp.bfloat16)


KEPT, BLANK, LANDED = 0, 1, 2


def keep_body(row_count, table_ref, pool_ref, key_ref, value_ref, after_ref, ready_ref, out_ref, mark_ref):
    mark_ref[...] = jnp.zeros_like(mark_ref)

    def fill(slot, carry):
        kind = table_ref[0, slot]
        req = table_ref[1, slot]

        @pl.when(kind == KEPT)
        def _():
            out_ref[0, slot] = pool_ref[0, slot]
            out_ref[1, slot] = pool_ref[1, slot]

        @pl.when(kind == BLANK)
        def _():
            blank = jnp.zeros(out_ref.shape[2:], out_ref.dtype)
            out_ref[0, slot] = blank
            out_ref[1, slot] = blank

        @pl.when((req >= 0) & (kind == KEPT))
        def _():
            first = table_ref[2, slot]
            for which, fresh_ref in ((0, key_ref), (1, value_ref)):
                out_ref[which, slot] = patched(
                    out_ref[which, slot], fresh_ref, row_count, req, first
                )

        return carry

    lax.fori_loop(0, table_ref.shape[1], fill, 0)


def moved(elements, flops=0):
    return pl.CostEstimate(flops=flops, bytes_accessed=2 * elements, transcendentals=0)


MARK = jax.ShapeDtypeStruct((CHUNK_ROWS, LANES), jnp.float32)


def place_kept(row_count, table, kv_pool, key_new, value_new, after, ready):
    vmem = pl.BlockSpec(memory_space=pltpu.VMEM)
    return pl.pallas_call(
        functools.partial(keep_body, row_count),
        out_shape=(jax.ShapeDtypeStruct(kv_pool.shape, kv_pool.dtype), MARK),
        in_specs=[pl.BlockSpec(memory_space=pltpu.SMEM)]
        + [vmem] * 3
        + [pl.BlockSpec(memory_space=pl.ANY)] * 2,
        out_specs=(vmem, vmem),
        compiler_params=pltpu.CompilerParams(vmem_limit_bytes=24 * 2**20),
        cost_estimate=moved(3 * kv_pool.size),
        name="place_kept",
    )(table, kv_pool, key_new, value_new, after, ready)


def land_body(
    row_count, capacity, table_ref, arrived_ref, key_ref, value_ref, begun_ref, out_ref, mark_ref,
    held_ref, load_sem, sem,
):
    places = table_ref.shape[1]
    senders = places // capacity

    def load_of(sender):
        span = pl.ds(2 * capacity * sender, 2 * capacity)
        return pltpu.make_async_copy(
            arrived_ref.at[span], held_ref.at[span], load_sem.at[sender]
        )

    for sender in range(senders):

        @pl.when(table_ref[5, sender * capacity] > 0)
        def _(sender=sender):
            load_of(sender).start()

    mark_ref[...] = jnp.zeros_like(mark_ref)
    for sender in range(senders):

        @pl.when(table_ref[5, sender * capacity] > 0)
        def _(sender=sender):
            load_of(sender).wait()
            for place in range(sender * capacity, (sender + 1) * capacity):
                plain = table_ref[0, place]

                @pl.when(plain >= 0)
                def _(place=place, plain=plain):
                    pltpu.make_async_copy(
                        held_ref.at[pl.ds(2 * place, 2)], out_ref.at[:, plain], sem
                    ).start()

    def patch(place, carry):
        req = table_ref[1, place]

        @pl.when(req >= 0)
        def _():
            first = table_ref[2, place]
            for which, fresh_ref in ((0, key_ref), (1, value_ref)):
                held_ref[2 * place + which] = patched(
                    held_ref[2 * place + which], fresh_ref, row_count, req, first
                )
            pltpu.make_async_copy(
                held_ref.at[pl.ds(2 * place, 2)], out_ref.at[:, table_ref[3, place]], sem
            ).start()

        return carry

    lax.fori_loop(0, places, patch, 0, unroll=4)
    group = held_ref.at[pl.ds(0, 2 * capacity)]
    wait_pages(group, held_ref.at[pl.ds(0, 2)], capacity, table_ref[4, 0], sem)


def place_landed(row_count, table, begun, arrived, key_new, value_new):
    slot_count, page_size, width = begun.shape[1:]
    capacity = arrived.shape[1] // 2
    vmem = pl.BlockSpec(memory_space=pltpu.VMEM)
    hbm = pl.BlockSpec(memory_space=pltpu.HBM)
    arrived = arrived.reshape(-1, page_size, width)
    return pl.pallas_call(
        functools.partial(land_body, row_count, capacity),
        out_shape=(jax.ShapeDtypeStruct(begun.shape, begun.dtype), MARK),
        in_specs=[pl.BlockSpec(memory_space=pltpu.SMEM), hbm, vmem, vmem, hbm],
        out_specs=(hbm, vmem),
        scratch_shapes=[
            pltpu.VMEM(arrived.shape, begun.dtype),
            pltpu.SemaphoreType.DMA((arrived.shape[0] // (2 * capacity),)),
            pltpu.SemaphoreType.DMA,
        ],
        input_output_aliases={4: 0},
        compiler_params=pltpu.CompilerParams(vmem_limit_bytes=32 * 2**20),
        cost_estimate=moved(3 * begun.size),
        name="place_landed",
    )(table, arrived, key_new, value_new, begun)


def split_parts(value):
    parts = []
    for _ in range(STAT_PARTS):
        part = value.astype(jnp.bfloat16).astype(jnp.float32)
        parts.append(part)
        value = value - part
    return parts


def attend_body(
    kv_count, group_size, seq_count, row_count,
    index_ref, query_ref, key_new_ref, value_new_ref, key_req_ref, pool_ref, *rest,
):
    out_refs, whole_ref, chunk_ref = rest[:-2], rest[-2], rest[-1]
    rows = query_ref.shape[0]
    width = kv_count * HD
    slot_count, page_size = pool_ref.shape[1:3]
    q_count = kv_count * group_size
    stack = rows * group_size
    row, held = row_ids(lax.broadcasted_iota(jnp.int32, (stack, 1), 0) % rows, row_count)
    row_req = jnp.where(held, row // STEPS, -2)
    new_row, new_held = row_ids(lax.broadcasted_iota(jnp.int32, (stack, rows), 1), row_count)
    mine = (row_req % seq_count) == index_ref[0]
    new_mask = (new_row // STEPS == row_req) & new_held & (new_row <= row) & mine
    stride = width // CHUNK_ROWS
    lane = lax.broadcasted_iota(jnp.int32, (rows, LANES), 1) % stride
    stats = jnp.zeros((rows, LANES), jnp.float32)
    for head in range(kv_count):
        cols = slice(head * HD, (head + 1) * HD)
        query = jnp.concatenate(
            [
                query_ref[:, (head * group_size + g) * HD : (head * group_size + g + 1) * HD]
                for g in range(group_size)
            ],
            axis=0,
        )
        contract = (((1,), (1,)), ((), ()))
        old_key = pool_ref[0, :, :, cols].reshape(slot_count * page_size, HD)
        old_value = pool_ref[1, :, :, cols].reshape(slot_count * page_size, HD)
        old = lax.dot_general(
            query, old_key, contract, preferred_element_type=jnp.float32
        ) * HD ** (-0.5)
        fresh = lax.dot_general(
            query, key_new_ref[:, cols], contract, preferred_element_type=jnp.float32
        ) * HD ** (-0.5)
        old_mask = key_req_ref[...] == row_req
        old = jnp.where(old_mask, old, NEG_FILL)
        fresh = jnp.where(new_mask, fresh, NEG_FILL)
        top = jnp.maximum(
            jnp.max(old, axis=1, keepdims=True), jnp.max(fresh, axis=1, keepdims=True)
        )
        old = jnp.where(old_mask, jnp.exp(old - top), 0.0)
        fresh = jnp.where(new_mask, jnp.exp(fresh - top), 0.0)
        total = jnp.sum(old, axis=1, keepdims=True) + jnp.sum(fresh, axis=1, keepdims=True)
        summed = jnp.dot(
            old.astype(jnp.bfloat16), old_value, preferred_element_type=jnp.float32
        ) + jnp.dot(
            fresh.astype(jnp.bfloat16), value_new_ref[:, cols], preferred_element_type=jnp.float32
        )
        summed = summed / jnp.where(total > 0.0, total, 1.0)
        parts = split_parts(top) + split_parts(total)
        for g in range(group_size):
            at = head * group_size + g
            own = slice(g * rows, (g + 1) * rows)
            whole_ref[:, at * HD : (at + 1) * HD] = summed[own]
            for k, part in enumerate(parts):
                stats = jnp.where(lane == k * q_count + at, part[own], stats)
    stats = jnp.concatenate([stats] * (width // LANES), axis=1)
    place = lax.broadcasted_iota(jnp.int32, (CHUNK_ROWS, width), 1) // stride
    chunk_row = lax.broadcasted_iota(jnp.int32, (CHUNK_ROWS, width), 0)
    for chunk in range(seq_count):
        span = slice(chunk * CHUNK_ROWS, (chunk + 1) * CHUNK_ROWS)
        line = jnp.sum(jnp.where(place == chunk_row, stats[span], 0.0), axis=0, keepdims=True)
        pieces = [whole_ref[span, g * width : (g + 1) * width] for g in range(group_size)]
        pieces[0] = jnp.where(chunk_row == row_count, line, pieces[0])
        chunk_ref[chunk] = jnp.concatenate(pieces, axis=0).astype(chunk_ref.dtype)
    inner = len(out_refs)
    own = index_ref[0] & (inner - 1)
    for shift, out_ref in enumerate(out_refs):
        for far in range(seq_count // inner):
            out_ref[far] = chunk_ref[far * inner + (own ^ shift)]


def attend(
    my_place, seq_count, inner, row_count, queries, key_new, value_new, key_req, kv_pool
):
    slot_count, page_size, width = kv_pool.shape[1:]
    kv_count = width // HD
    rows, q_width = queries.shape
    group_size = q_width // width
    assert group_size * CHUNK_ROWS == page_size and row_count < CHUNK_ROWS
    assert 2 * STAT_PARTS * kv_count * group_size <= width // CHUNK_ROWS
    smem = pl.BlockSpec(memory_space=pltpu.SMEM)
    vmem = pl.BlockSpec(memory_space=pltpu.VMEM)
    return pl.pallas_call(
        functools.partial(attend_body, kv_count, group_size, seq_count, row_count),
        out_shape=(jax.ShapeDtypeStruct((seq_count // inner, page_size, width), jnp.bfloat16),)
        * inner,
        in_specs=[smem] + [vmem] * 5,
        out_specs=(vmem,) * inner,
        scratch_shapes=[
            pltpu.VMEM((rows, q_width), jnp.float32),
            pltpu.VMEM((seq_count, page_size, width), jnp.bfloat16),
        ],
        compiler_params=pltpu.CompilerParams(vmem_limit_bytes=48 * 2**20),
        cost_estimate=moved(2 * kv_pool.size, 4 * rows * q_width * slot_count * page_size),
        name="attend",
    )(
        my_place, queries, key_new, value_new, key_req, kv_pool
    )


def merge_units(units, q_count, row_count):
    width = units[0].shape[1]
    stride = width // CHUNK_ROWS
    place = lax.broadcasted_iota(jnp.int32, (CHUNK_ROWS, width), 1) // stride
    chunk_row = lax.broadcasted_iota(jnp.int32, (CHUNK_ROWS, width), 0)
    tops, sums = [], []
    for unit in units:
        stats = jnp.where(place == chunk_row, unit[row_count : row_count + 1], 0.0)
        shift = width // 2
        while shift >= stride:
            stats = stats + pltpu.roll(stats, shift, 1)
            shift //= 2
        stats = stats[:, :LANES]
        pieces = [stats] + [
            pltpu.roll(stats, LANES - k * q_count, 1) for k in range(1, 2 * STAT_PARTS)
        ]
        tops.append(sum(pieces[1:STAT_PARTS], pieces[0]))
        sums.append(sum(pieces[STAT_PARTS + 1 :], pieces[STAT_PARTS]))
    lane = lax.broadcasted_iota(jnp.int32, (CHUNK_ROWS, LANES), 1)
    tops = [jnp.where(lane < q_count, top, 0.0) for top in tops]
    sums = [jnp.where(lane < q_count, total, 0.0) for total in sums]
    peak = functools.reduce(jnp.maximum, tops)
    shares = [total * jnp.exp(top - peak) for top, total in zip(tops, sums)]
    whole = sum(shares[1:], shares[0])
    inverse = 1.0 / jnp.where(whole > 0.0, whole, 1.0)
    shares = [share * inverse for share in shares]
    heads = []
    for head in range(q_count):
        half = head * HD // width
        at = head * HD - half * width
        acc = jnp.zeros((CHUNK_ROWS, HD), jnp.float32)
        for unit, share in zip(units, shares):
            block = unit[half * CHUNK_ROWS : (half + 1) * CHUNK_ROWS, at : at + HD]
            acc = acc + block * share[:, head : head + 1]
        heads.append(acc)
    return heads, peak, whole


def merge_body(q_count, row_count, index_ref, mark_ref, weight_ref, *rest):
    rest, near_ref, held_ref, load_sem = rest[:-3], rest[-3], rest[-2], rest[-1]
    load = pltpu.make_async_copy(weight_ref, near_ref, load_sem)
    load.start()
    far_count = rest[0].shape[0]
    part_refs, out_refs = rest[:-far_count], rest[-far_count:]
    width = held_ref.shape[2]
    stride = width // CHUNK_ROWS
    place = lax.broadcasted_iota(jnp.int32, (CHUNK_ROWS, width), 1) // stride
    chunk_row = lax.broadcasted_iota(jnp.int32, (CHUNK_ROWS, width), 0)
    for far in range(far_count):
        units = [part_ref[far].astype(jnp.float32) for part_ref in part_refs]
        heads, peak, whole = merge_units(units, q_count, row_count)
        stats = jnp.zeros((CHUNK_ROWS, LANES), jnp.float32)
        for k, part in enumerate(split_parts(peak) + split_parts(whole)):
            stats = stats + (pltpu.roll(part, k * q_count, 1) if k else part)
        shift = stride
        while shift < LANES:
            stats = stats + pltpu.roll(stats, shift, 1)
            shift *= 2
        stats = jnp.concatenate([stats] * (width // LANES), axis=1)
        line = jnp.sum(jnp.where(place == chunk_row, stats, 0.0), axis=0, keepdims=True)
        numerators = jnp.concatenate(heads, axis=1)
        pieces = [
            numerators[:, g * width : (g + 1) * width]
            for g in range(numerators.shape[1] // width)
        ]
        pieces[0] = jnp.where(chunk_row == row_count, line, pieces[0])
        held_ref[far] = jnp.concatenate(pieces, axis=0).astype(held_ref.dtype)
    own = index_ref[0] // len(part_refs)
    for shift, out_ref in enumerate(out_refs):
        out_ref[...] = held_ref[own ^ shift]
    load.wait()


def merge(my_place, mark, w_out, parts, q_count, row_count):
    far_count, page_size, width = parts[0].shape
    vmem = pl.BlockSpec(memory_space=pltpu.VMEM)
    unit = jax.ShapeDtypeStruct((page_size, width), jnp.bfloat16)
    return pl.pallas_call(
        functools.partial(merge_body, q_count, row_count),
        out_shape=(unit,) * far_count + (pltpu.VMEM(w_out.shape, w_out.dtype),),
        in_specs=[
            pl.BlockSpec(memory_space=pltpu.SMEM),
            pl.BlockSpec(memory_space=pl.ANY),
            pl.BlockSpec(memory_space=pltpu.HBM),
        ]
        + [vmem] * len(parts),
        out_specs=(vmem,) * (far_count + 1),
        scratch_shapes=[
            pltpu.VMEM((far_count, page_size, width), jnp.bfloat16),
            pltpu.SemaphoreType.DMA,
        ],
        compiler_params=pltpu.CompilerParams(vmem_limit_bytes=24 * 2**20),
        cost_estimate=moved(3 * 2**20),
        name="merge",
    )(my_place, mark, w_out, *parts)


def combine_body(q_count, row_count, tp_count, index_ref, *refs):
    part_refs, weight_ref, out_refs = refs[: -1 - tp_count], refs[-1 - tp_count], refs[-tp_count:]
    units = [part_ref[...].astype(jnp.float32) for part_ref in part_refs]
    heads, _, _ = merge_units(units, q_count, row_count)
    attended = jnp.concatenate([head.astype(jnp.bfloat16) for head in heads], axis=1)
    total = jnp.dot(attended, weight_ref[...], preferred_element_type=jnp.float32)
    width = total.shape[1] // tp_count
    blocks = [total[:, k * width : (k + 1) * width] for k in range(tp_count)]
    for shift, out_ref in enumerate(out_refs):
        chosen = blocks[0]
        for k in range(1, tp_count):
            chosen = jnp.where((index_ref[1] ^ shift) == k, blocks[k], chosen)
        out_ref[...] = chosen.astype(out_ref.dtype)


def combine(my_place, tp_count, parts, w_near, row_count):
    vmem = pl.BlockSpec(memory_space=pltpu.VMEM)
    block = jax.ShapeDtypeStruct((CHUNK_ROWS, w_near.shape[1] // tp_count), jnp.bfloat16)
    return pl.pallas_call(
        functools.partial(combine_body, w_near.shape[0] // HD, row_count, tp_count),
        out_shape=(block,) * tp_count,
        in_specs=[pl.BlockSpec(memory_space=pltpu.SMEM)] + [vmem] * (len(parts) + 1),
        out_specs=(vmem,) * tp_count,
        compiler_params=pltpu.CompilerParams(vmem_limit_bytes=24 * 2**20),
        cost_estimate=moved(2 * w_near.size),
        name="combine",
    )(my_place, *parts, w_near)


def close_body(mark_ref, *refs):
    part_refs, out_ref = refs[:-1], refs[-1]
    total = part_refs[0][...].astype(jnp.float32)
    for part_ref in part_refs[1:]:
        total = total + part_ref[...].astype(jnp.float32)
    out_ref[...] = total[: out_ref.shape[0]].astype(out_ref.dtype)


def close(mark, parts, row_count):
    vmem = pl.BlockSpec(memory_space=pltpu.VMEM)
    return pl.pallas_call(
        close_body,
        out_shape=jax.ShapeDtypeStruct((row_count, parts[0].shape[1]), jnp.bfloat16),
        in_specs=[pl.BlockSpec(memory_space=pl.ANY)] + [vmem] * len(parts),
        out_specs=vmem,
        compiler_params=pltpu.CompilerParams(vmem_limit_bytes=16 * 2**20),
        name="close",
    )(mark, *parts)


def swap_all(parts, step, count, axis="seq"):
    pairs = [[(i, i ^ (k * step)) for i in range(count)] for k in range(len(parts))]
    return [parts[0]] + [lax.ppermute(parts[k], axis, pairs[k]) for k in range(1, len(parts))]


def length_of(lengths, request):
    hot = request[..., None] == jnp.arange(lengths.shape[0], dtype=jnp.int32)
    return jnp.sum(jnp.where(hot, lengths, 0), axis=-1)


def slot_tables(notes, row_count, my_index, capacity, slot_owner, slot_dest, lengths, page_size):
    seq_count = notes.shape[0]
    slot_count = slot_dest.shape[0]
    dest, req, page = read_notes(notes, row_count, slot_count)
    inner = dest - my_index * slot_count
    to_me = (inner >= 0) & (inner < slot_count)
    rank = jnp.cumsum(to_me.astype(jnp.int32), axis=1) - 1
    match = to_me[:, None, :] & (
        rank[:, None, :] == jnp.arange(capacity, dtype=jnp.int32)[None, :, None]
    )

    def pick(value):
        return jnp.sum(jnp.where(match, value[:, None, :] + 1, 0), axis=2).reshape(-1) - 1

    def fresh(request, held_page):
        first = length_of(lengths, request) - held_page * page_size
        hit = (request >= 0) & (first > -STEPS) & (first < page_size)
        return jnp.where(hit, request, -1), first

    slot = pick(inner)
    new_req, first = fresh(pick(req), pick(page))
    count = jnp.broadcast_to(jnp.sum((slot >= 0).astype(jnp.int32)), slot.shape)
    sends = jnp.repeat(jnp.sum(to_me.astype(jnp.int32), axis=1), capacity)
    plain = jnp.where(new_req < 0, slot, -1)
    by_place = jnp.stack([plain, new_req, first, slot, count, sends])
    landed = jnp.any(slot[None, :] == jnp.arange(slot_count, dtype=jnp.int32)[:, None], axis=1)
    stays = slot_dest < 0
    kind = jnp.where(landed, LANDED, jnp.where(stays, KEPT, BLANK))
    held_req = jnp.where(kind == KEPT, slot_owner[:, 0], -1)
    by_slot = jnp.stack([kind, *fresh(held_req, slot_owner[:, 1])])
    return by_slot, by_place


def local(tokens, norm_gain, w_query, w_key_value, w_out, kv_pool, slot_owner, slot_dest, lengths):
    seq_count = lax.axis_size("seq")
    tp_count = lax.axis_size("tp")
    my_index = lax.axis_index("seq")
    my_place = jnp.stack([my_index, lax.axis_index("tp")]).astype(jnp.int32)
    row_count, token_width = tokens.shape
    slot_count, page_size = kv_pool.shape[1:3]
    capacity = -(-slot_count // seq_count)

    inner = 1 << ((seq_count.bit_length() - 1) // 2)
    note = make_note(tokens, slot_owner, slot_dest)
    along = swap_all([note] * (seq_count // inner), inner, seq_count)
    outgoing = pack_pages(kv_pool, slot_dest, seq_count, capacity)
    outgoing, along, lengths = lax.optimization_barrier((outgoing, along, lengths))
    notes = sort_notes(my_place, swap_all([jnp.stack(along)] * inner, 1, seq_count))
    arrived = lax.all_to_all(outgoing, "seq", split_axis=0, concat_axis=0, tiled=True)

    seq_tokens = notes[:, :CHUNK_ROWS].reshape(seq_count * CHUNK_ROWS, token_width)
    all_tokens = lax.all_gather(seq_tokens, "tp", axis=1, tiled=True)
    queries, key_new, value_new = project_rows(
        all_tokens, row_count, norm_gain, w_query, w_key_value, lengths
    )
    by_slot, by_place = slot_tables(
        notes, row_count, my_index, capacity, slot_owner, slot_dest, lengths, page_size
    )
    key_wide, value_wide = key_new.astype(jnp.float32), value_new.astype(jnp.float32)
    owner_req = slot_owner[:, 0]
    base_len = length_of(lengths, owner_req)
    position = slot_owner[:, 1][:, None] * page_size + jnp.arange(page_size, dtype=jnp.int32)[None, :]
    key_req = jnp.where(position < base_len[:, None], owner_req[:, None], -1).reshape(1, -1)
    payload = attend(
        my_place, seq_count, inner, row_count, queries, key_new, value_new, key_req, kv_pool
    )
    begun, mark = place_kept(row_count, by_slot, kv_pool, key_wide, value_wide, payload[0], by_place)
    near = swap_all(payload, 1, seq_count)
    *merged, w_near = merge(my_place, mark, w_out, near, w_query.shape[1] // HD, row_count)
    far = swap_all(merged, inner, seq_count)
    columns = combine(my_place, tp_count, far, w_near, row_count)
    columns = swap_all(columns, 1, tp_count, "tp")
    kv_moved, mark = place_landed(row_count, by_place, begun, arrived, key_wide, value_wide)
    attn_out = close(mark, columns, row_count)
    return (attn_out, kv_moved)


def solution(mesh):
    in_specs = (
        P("seq", "tp"),
        P(),
        P(None, "tp"),
        P(None, None, "tp"),
        P("tp", None),
        P(None, "seq", None, "tp"),
        P("seq", None),
        P("seq"),
        P(),
    )
    out_specs = (P("seq", "tp"), P(None, "seq", None, "tp"))
    return jax.shard_map(local, mesh=mesh, in_specs=in_specs, out_specs=out_specs, check_vma=False)
```
